32 devices in a mesh: groups: 2 (over y), cells: 4 (over z), genes: 2 (over x), sub: 2 (over core).
Axes of the slice: x: 2, y: 2, z: 4, core: 2. Of those that a mesh axis runs over, the one named last changes fastest.
Arguments:
- counts: int32 [8192, 16384], P(('groups', 'cells'), ('genes', 'sub')), parts along dimension 0, may hold values from 0 to 33, as said below
- start_block: float32 [16384, 64], P(('genes', 'sub')), may hold values from -6 to 6
Outputs:
- scores: float32 [8192, 64], P(('groups', 'cells')), parts along dimension 0
- loadings: float32 [32768, 64], P(('groups', 'genes', 'sub')), parts along dimension 0
- ritz: float32 [128, 64], P('groups'), parts along dimension 0
The draws below stay inside these ranges and needn't reach their ends.
There are 2 independent parts, one for each index of `groups`. The reference program is written for one: setup_inputs(seed, part) draws one part's arguments, and reference() takes and returns one part's arrays. A program takes and returns all parts, laid end to end along the dimension named above; an argument that names none is the same for every part. Nothing has to cross between parts.
Inputs may be any that keep to these rules, and one draw needn't show every extreme that they name: `counts`: every cell has at least one positive count.
All inputs are finite; a program needn't handle non-finite values.
Results may differ from the reference program's by a relative error of at most 0.00026.
Values sent between devices are 32-bit elements; how exact they have to be, the bound alone decides.
No kernel may reach another device: no remote copies, remote signals or barrier semaphores. Data moves between devices by JAX's collectives and lax.ppermute only.
A program may use at most 64 MiB of HBM per device.

```python
import jax
import jax.numpy as jnp
from jax import lax

GENES = 16384
RANK = 64
CELLS = 4096


def draw_counts(key, part):
    key = jax.random.fold_in(key, 7)
    first, second, third, fourth, fifth, sixth = jax.random.split(key, 6)
    gene_pos = jnp.arange(GENES, dtype=jnp.int32)
    cell_pos = jnp.arange(CELLS, dtype=jnp.int32)
    gene_top = 1 + 6 * gene_pos // GENES + jax.random.randint(first, (GENES,), 0, 3)
    depth = 1 + 3 * cell_pos // CELLS + jax.random.randint(second, (CELLS,), 0, 2)
    ceiling = depth[:, None] * gene_top[None, :] + 1
    drawn = jax.random.randint(third, (CELLS, GENES), 0, ceiling)
    picked = jax.random.randint(fourth, (CELLS, 1), 0, GENES)
    result = drawn + (gene_pos[None, :] == picked).astype(jnp.int32)
    top_cell = jax.random.randint(fifth, (), 0, CELLS)
    top_gene = jax.random.randint(sixth, (), 0, GENES)
    marked = (cell_pos[:, None] == top_cell) & (gene_pos[None, :] == top_gene)
    return jnp.where(marked, jnp.int32(33), result).astype(jnp.int32)


def shard_levels(key, extent, shards, least, largest):
    level, own = 1.0, jax.random.fold_in(key, 6)
    for dim, shards_of in shards:
        draws = jnp.exp(jax.random.uniform(jax.random.fold_in(own, dim), (shards_of,), jnp.float32, least / len(shards), largest / len(shards)))
        level = level * jnp.repeat(draws, extent[dim] // shards_of).reshape([-1 if axis == dim else 1 for axis in range(len(extent))])
    return level


def bell_draw(stream_key, dims, spread, bound, shards=(), held_as=jnp.bfloat16):
    level = shard_levels(stream_key, dims, shards, -0.22, 0.18) if shards else 1.0
    array = jax.random.normal(stream_key, dims, jnp.float32) * spread * level
    return jnp.minimum(jnp.maximum(array, -bound), bound).astype(held_as)


def setup_inputs(seed: int = 0, part: int = 0) -> dict:
    arg_keys = jax.random.split(jax.random.key(seed), 3)
    part_splits = jax.random.split(jax.random.fold_in(arg_keys[2], part), 3)
    counts = draw_counts(jax.random.fold_in(jax.random.fold_in(arg_keys[2], part), 71), part)
    start_block = bell_draw(arg_keys[1], (GENES, RANK), 1.0, 6.0, ((0, 4),), jnp.float32)
    return {"counts": counts, "start_block": start_block}


def reference(counts, start_block):
    hi = lax.Precision.HIGHEST
    values = counts.astype(jnp.float32)
    library = lax.optimization_barrier(jnp.sum(values, axis=1))
    logged = jnp.log1p(values * (10000.0 / library)[:, None])
    ncells = logged.shape[0]
    mean = lax.optimization_barrier(jnp.sum(logged, axis=0)) / ncells
    meansq = lax.optimization_barrier(jnp.sum(logged * logged, axis=0)) / ncells
    scale = 1.0 / jnp.sqrt(meansq - mean * mean + 1e-05)
    standard = (logged - mean[None, :]) * scale[None, :]
    sketch = jnp.dot(standard.astype(jnp.float32), start_block.astype(jnp.float32), precision=hi, preferred_element_type=jnp.float32)
    gram = jnp.dot(sketch.T.astype(jnp.float32), sketch.astype(jnp.float32), precision=hi, preferred_element_type=jnp.float32)
    lower = jnp.linalg.cholesky(gram)
    ortho = lax.linalg.triangular_solve(lower, sketch, left_side=False, lower=True, transpose_a=True)
    loadings = jnp.dot(standard.T.astype(jnp.float32), ortho.astype(jnp.float32), precision=hi, preferred_element_type=jnp.float32)
    ritz = jnp.dot(loadings.T.astype(jnp.float32), loadings.astype(jnp.float32), precision=hi, preferred_element_type=jnp.float32) / GENES
    scores = ortho * jnp.sqrt(jnp.float32(ncells))
    return (scores, loadings, ritz)
```

```python
import functools

import jax
import jax.numpy as jnp
from jax import lax
from jax.experimental import pallas as pl
from jax.experimental.pallas import tpu as pltpu
from jax.sharding import PartitionSpec as P

F32 = jnp.float32
BF16 = jnp.bfloat16
HI = lax.Precision.HIGHEST
VM = pl.BlockSpec(memory_space=pltpu.VMEM)
SM = pl.BlockSpec(memory_space=pltpu.SMEM)
ANY = pl.BlockSpec(memory_space=pl.ANY)
MIB = 1 << 20
NT = (((1,), (1,)), ((), ()))
NN = (((1,), (0,)), ((), ()))


def params(mib=16):
    return pltpu.CompilerParams(vmem_limit_bytes=mib * MIB)


def vmem(x):
    return pltpu.with_memory_space_constraint(x, pltpu.VMEM)


def cost(flops, nbytes):
    return pl.CostEstimate(flops=int(flops), bytes_accessed=int(nbytes), transcendentals=0)


def swap(x, axis, k=1):
    size = lax.axis_size(axis)
    return lax.ppermute(x, axis, [(i, i ^ k) for i in range(size)])


def is_pow2(size):
    return size & (size - 1) == 0


def sum_over(x, axes):
    for axis in axes:
        size = lax.axis_size(axis)
        if not is_pow2(size):
            x = lax.psum(x, axis)
        elif size == 4:
            a, b, c = swap(x, axis, 1), swap(x, axis, 2), swap(x, axis, 3)
            x = (x + a) + (b + c)
        else:
            k = 1
            while k < size:
                x = x + swap(x, axis, k)
                k *= 2
    return x


def totals_kernel(bm, nbuf, counts, compact, total, buf, sem):
    m, n = counts.shape
    steps = m // bm

    def fetch(i):
        return pltpu.make_async_copy(
            counts.at[pl.ds(i * bm, bm), :], buf.at[i % nbuf], sem.at[i % nbuf]
        )

    for i in range(min(nbuf, steps)):
        fetch(i).start()
    for i in range(steps):
        fetch(i).wait()
        slot = i % nbuf

        def tile(t, acc, slot=slot, i=i):
            at = pl.ds(pl.multiple_of(t * 128, 128), 128)
            x = buf[slot, :, at].astype(F32)
            compact[pl.ds(i * bm, bm), at] = x.astype(BF16)
            return acc + x

        acc = lax.fori_loop(0, n // 128, tile, jnp.zeros((bm, 128), F32), unroll=4)
        total[:, pl.ds(i * bm, bm)] = jnp.sum(acc.T, axis=0, keepdims=True)
        if i + nbuf < steps:
            fetch(i + nbuf).start()


def column(library, factor, m):
    for t in range(m // 128):
        row = 10000.0 / library[:, t * 128 : (t + 1) * 128]
        factor[t * 128 : (t + 1) * 128, :] = jnp.broadcast_to(row, (128, 128)).T


def logged_block(compact, factor, rows, cols, width):
    x = compact[rows, cols].astype(F32)
    s = factor[rows, :]
    s = jnp.concatenate([s] * (width // 128), axis=1)
    return jnp.log(1.0 + x * s)


def stats_kernel(compact, library, stats, factor):
    m, n = compact.shape
    column(library, factor, m)
    width, bm = 512, 64

    def over_cols(t, carry):
        cols = pl.ds(pl.multiple_of(t * width, width), width)

        def over_rows(r, acc):
            rows = pl.ds(pl.multiple_of(r * bm, bm), bm)
            y = logged_block(compact, factor, rows, cols, width)
            parts = y.reshape(bm // 8, 8, width)
            return acc[0] + jnp.sum(parts, axis=0), acc[1] + jnp.sum(parts * parts, axis=0)

        zero = jnp.zeros((8, width), F32)
        one, two = lax.fori_loop(0, m // bm, over_rows, (zero, zero))
        stats[0:1, cols] = jnp.sum(one, axis=0, keepdims=True)
        stats[1:2, cols] = jnp.sum(two, axis=0, keepdims=True)
        return carry

    lax.fori_loop(0, n // width, over_cols, 0)


def split_kernel(compact, library, high, low, factor):
    m, n = compact.shape
    column(library, factor, m)
    width, bm = 512, 64

    def over_rows(r, carry):
        rows = pl.ds(pl.multiple_of(r * bm, bm), bm)

        def over_cols(t, c):
            cols = pl.ds(pl.multiple_of(t * width, width), width)
            y = logged_block(compact, factor, rows, cols, width)
            h = y.astype(BF16)
            high[rows, cols] = h
            low[rows, cols] = (y - h.astype(F32)).astype(BF16)
            return c

        return lax.fori_loop(0, n // width, over_cols, carry)

    lax.fori_loop(0, m // bm, over_rows, 0)


def mean_scale(stats, ncells):
    mean = stats[0:1, :] / ncells
    meansq = stats[1:2, :] / ncells
    return mean, 1.0 / jnp.sqrt(meansq - mean * mean + 1e-05)


def two_parts(x):
    h = x.astype(BF16)
    return h, (x - h.astype(F32)).astype(BF16)


def sketch_kernel(ncells, high, low, start_t, stats, part, weight):
    m, n = high.shape
    rank = start_t.shape[0]
    mean, scale = mean_scale(stats[...], ncells)
    w = start_t[...] * scale
    shift = jnp.sum(w * mean, axis=1, keepdims=True)
    h, l = two_parts(w)
    weight[...] = jnp.concatenate([h, l], axis=0).T
    bm = min(256, m // 2)
    for r in range(m // bm):
        rows = slice(r * bm, (r + 1) * bm)
        acc = jnp.dot(high[rows, :], weight[...], preferred_element_type=F32)
        acc = acc + jnp.dot(low[rows, :], weight[...], preferred_element_type=F32)
        acc = acc.T
        half, at = divmod(r * bm, m // 2)
        part[half, :, at : at + bm] = acc[:rank] + acc[rank:] - shift


def prep_kernel(first, own, other, sketch, packed, colsum, gram):
    rank, half = own.shape
    mine, theirs = own[...], other[...]
    left = jnp.where(first[0] == 1, mine, theirs)
    right = jnp.where(first[0] == 1, theirs, mine)
    s = jnp.concatenate([left, right], axis=1)
    sketch[...] = s
    h, l = two_parts(s)
    packed[...] = jnp.concatenate([h, l], axis=0)
    colsum[...] = jnp.broadcast_to(jnp.sum(s, axis=1, keepdims=True), colsum.shape)
    gram[...] = lax.dot_general(s, s, NT, precision=HI, preferred_element_type=F32)


def eliminate_kernel(k0, k1, last, state, out):
    rank = state.shape[0]
    a = state[...]
    row = lax.broadcasted_iota(jnp.int32, (rank, 1), 0)
    for k in range(k0, k1):
        pivot = a[k : k + 1, :]
        f = a[:, k : k + 1] * (1.0 / a[k : k + 1, k : k + 1])
        a = a - jnp.where(row > k, f, 0.0) * pivot
    if last:
        lane = lax.broadcasted_iota(jnp.int32, (rank, rank), 1)
        diag = jnp.sum(jnp.where(lane == row, a[:, :rank], 0.0), axis=1, keepdims=True)
        out[...] = a[:, rank:] * (1.0 / jnp.sqrt(diag))
    else:
        out[...] = a


def scores_kernel(ncells, sketch, inverse, scores):
    s = lax.dot_general(inverse[...], sketch[...], NN, precision=HI, preferred_element_type=F32)
    scores[...] = (s * (float(ncells) ** 0.5)).T


def z_chunk(ncells, c0, nc, packed, colsum, high, low, stats):
    rank = colsum.shape[0]
    cols = slice(c0, c0 + nc)
    z = jnp.dot(packed[...], high[:, cols], preferred_element_type=F32)
    z = z + jnp.dot(packed[...], low[:, cols], preferred_element_type=F32)
    mean, scale = mean_scale(stats[:, cols], ncells)
    return (z[:rank] + z[rank:] - colsum[:, 0:1] * mean) * scale


def product_kernel(ncells, c0, nc, token, packed, colsum, high, low, stats, z, token_out):
    z[...] = z_chunk(ncells, c0, nc, packed, colsum, high, low, stats)
    token_out[...] = token[...]


def finish(value, inverse, square, square_out, stage):
    l = lax.dot_general(inverse[...], value, NN, precision=HI, preferred_element_type=F32)
    square_out[...] = square[...] + lax.dot_general(
        l, l, NT, precision=HI, preferred_element_type=F32
    )
    stage[...] = l.T


def body(counts, start_block):
    m, n = counts.shape
    rank = start_block.shape[1]
    cells = lax.axis_size("cells")
    ncells = m * cells
    genes = n * lax.axis_size("genes") * lax.axis_size("sub")

    bm, nbuf = 128, 4
    compact, total = pl.pallas_call(
        functools.partial(totals_kernel, bm, nbuf),
        name="totals",
        out_shape=(pltpu.VMEM((m, n), BF16), jax.ShapeDtypeStruct((1, m), F32)),
        in_specs=[ANY],
        out_specs=(VM, VM),
        scratch_shapes=[pltpu.VMEM((nbuf, bm, n), jnp.int32), pltpu.SemaphoreType.DMA((nbuf,))],
        compiler_params=params(),
        cost_estimate=cost(0, 24 * m * n),
    )(counts)
    library = sum_over(total, ("sub", "genes"))
    start_t = start_block.T

    stats = pl.pallas_call(
        stats_kernel,
        name="stats",
        out_shape=jax.ShapeDtypeStruct((2, n), F32),
        in_specs=[VM, VM],
        out_specs=VM,
        scratch_shapes=[pltpu.VMEM((m, 128), F32)],
        compiler_params=params(),
        cost_estimate=cost(0, 20 * m * n),
    )(vmem(compact), library)
    stats = sum_over(stats, ("cells",))

    high, low = pl.pallas_call(
        split_kernel,
        name="split",
        out_shape=(pltpu.VMEM((m, n), BF16), pltpu.VMEM((m, n), BF16)),
        in_specs=[VM, VM],
        out_specs=(VM, VM),
        scratch_shapes=[pltpu.VMEM((m, 128), F32)],
        compiler_params=params(),
        cost_estimate=cost(0, 20 * m * n),
    )(vmem(compact), library)

    part = pl.pallas_call(
        functools.partial(sketch_kernel, ncells),
        name="sketch",
        out_shape=jax.ShapeDtypeStruct((2, rank, m // 2), F32),
        in_specs=[VM] * 4,
        out_specs=VM,
        scratch_shapes=[pltpu.VMEM((n, 2 * rank), BF16)],
        compiler_params=params(),
        cost_estimate=cost(8 * m * n * 64, 4 * m * n),
    )(vmem(high), vmem(low), start_t, stats)

    if lax.axis_size("sub") == 2:
        me = lax.axis_index("sub")
        own = lax.dynamic_index_in_dim(part, me, 0, keepdims=False)
        away = lax.dynamic_index_in_dim(part, 1 - me, 0, keepdims=False)
        own = own + swap(away, "sub")
        own = sum_over(own, ("genes",))
        other = swap(own, "sub")
        first = (me == 0).astype(jnp.int32).reshape(1)
    else:
        part = sum_over(part, ("sub", "genes"))
        own, other = part[0], part[1]
        first = jnp.ones((1,), jnp.int32)

    sketch, packed, colsum, gram = pl.pallas_call(
        prep_kernel,
        name="prep",
        out_shape=(
            jax.ShapeDtypeStruct((rank, m), F32),
            jax.ShapeDtypeStruct((2 * rank, m), BF16),
            jax.ShapeDtypeStruct((rank, 128), F32),
            jax.ShapeDtypeStruct((rank, rank), F32),
        ),
        in_specs=[SM, VM, VM],
        out_specs=(VM,) * 4,
        compiler_params=params(),
        cost_estimate=cost(12 * m * rank * rank, 16 * m * rank),
    )(first, own, other)

    gram = sum_over(gram, ("cells",))
    state = jnp.concatenate([gram, jnp.eye(rank, dtype=F32)], axis=1)
    steps = 16
    for k in range(0, rank, steps):
        last = k + steps == rank
        state = pl.pallas_call(
            functools.partial(eliminate_kernel, k, k + steps, last),
            name="eliminate",
            out_shape=jax.ShapeDtypeStruct((rank, rank if last else 2 * rank), F32),
            in_specs=[VM],
            out_specs=VM,
            compiler_params=params(),
            cost_estimate=cost(0, 8 * MIB),
        )(state)
    inverse = state

    scores = pl.pallas_call(
        functools.partial(scores_kernel, ncells),
        name="scores",
        out_shape=jax.ShapeDtypeStruct((m, rank), F32),
        in_specs=[VM, VM],
        out_specs=VM,
        compiler_params=params(),
        cost_estimate=cost(12 * m * rank * rank, 2 * MIB),
    )(sketch, inverse)

    chunks = 8 if n % 1024 == 0 else 1
    nc = n // chunks
    token = jnp.zeros((8, 128), F32)
    square = jnp.zeros((rank, rank), F32)
    loadings = None
    line = cells == 4 and lax.axis_size("sub") == 2

    def product(c, token):
        return pl.pallas_call(
            functools.partial(product_kernel, ncells, c * nc, nc),
            name="product",
            out_shape=(
                jax.ShapeDtypeStruct((rank, nc), F32),
                jax.ShapeDtypeStruct((8, 128), F32),
            ),
            in_specs=[VM] * 6,
            out_specs=(VM, VM),
            compiler_params=params(),
            cost_estimate=cost(8 * m * nc * 64, 4 * m * nc),
        )(token, packed, colsum, vmem(high), vmem(low), stats)

    def final(c, values, square, loadings):
        def kernel(*refs):
            refs = list(refs)
            edge = refs.pop(0)
            vals = [refs.pop(0) for _ in values]
            inv, sq = refs.pop(0), refs.pop(0)
            if loadings is not None:
                refs.pop(0)
            sq_out, out, stage, sem = refs
            v = vals[0][...]
            if len(vals) > 1:
                v = jnp.where(edge[0] == 1, vals[1][...], v)
            finish(v, inv, sq, sq_out, stage)
            copy = pltpu.make_async_copy(stage, out.at[pl.ds(c * nc, nc), :], sem)
            copy.start()
            copy.wait()

        extra = [] if loadings is None else [loadings]
        return pl.pallas_call(
            kernel,
            name="final",
            out_shape=(
                jax.ShapeDtypeStruct((rank, rank), F32),
                jax.ShapeDtypeStruct((n, rank), F32),
            ),
            in_specs=[SM] + [VM] * (len(values) + 2) + [ANY] * len(extra),
            out_specs=(VM, ANY),
            scratch_shapes=[pltpu.VMEM((nc, rank), F32), pltpu.SemaphoreType.DMA],
            input_output_aliases={} if loadings is None else {len(values) + 3: 1},
            compiler_params=params(),
            cost_estimate=cost(12 * rank * rank * nc * 2, 2 * MIB),
        )(edge, *values, inverse, square, *extra)

    if line:
        where = lax.axis_index("cells")
        end = (where == 0) | (where == cells - 1)
        edge = end.astype(jnp.int32).reshape(1)
        pairs = [(0, 1), (1, 0), (2, 3), (3, 2)]
        middle = [(2, 4), (4, 2), (3, 5), (5, 3), (0, 1), (1, 0), (6, 7), (7, 6)]
        lag = 2
        z, s, t, back = ([None] * chunks for _ in range(4))
        for slot in range(chunks + 3 * lag):
            a, b, c, d = slot, slot - lag, slot - 2 * lag, slot - 3 * lag
            if a < chunks:
                z[a], token = product(a, token)
            give = None
            if 0 <= c < chunks:
                t[c] = s[c] + t[c]
            if a < chunks and 0 <= c:
                give = jnp.where(end, z[a], t[c])
            elif a < chunks:
                give = z[a]
            elif c < chunks:
                give = t[c]
            if give is not None:
                got = lax.ppermute(give, "cells", pairs)
                if a < chunks:
                    s[a] = got
                if 0 <= c < chunks:
                    back[c] = got
            if 0 <= b < chunks:
                s[b] = z[b] + s[b]
                t[b] = lax.ppermute(s[b], ("cells", "sub"), middle)
            if 0 <= d < chunks:
                square, loadings = final(d, (t[d], back[d]), square, loadings)
    else:
        edge = jnp.zeros((1,), jnp.int32)
        for c in range(chunks):
            z, token = product(c, token)
            square, loadings = final(c, (lax.psum(z, "cells"),), square, loadings)

    ritz = sum_over(square, ("sub", "genes")) / genes
    return (scores, loadings, ritz)


def solution(mesh):
    placed = (P(("groups", "cells"), ("genes", "sub")), P(("genes", "sub"), None))
    return jax.shard_map(
        body,
        mesh=mesh,
        in_specs=placed,
        out_specs=(
            P(("groups", "cells"), None),
            P(("groups", "genes", "sub"), None),
            P("groups", None),
        ),
        check_vma=False,
    )
```

```python
import functools

import jax
import jax.numpy as jnp
from jax import lax
from jax.experimental import pallas as pl
from jax.experimental.pallas import tpu as pltpu
from jax.sharding import PartitionSpec as P

F32 = jnp.float32
BF16 = jnp.bfloat16
HI = lax.Precision.HIGHEST
VM = pl.BlockSpec(memory_space=pltpu.VMEM)
SM = pl.BlockSpec(memory_space=pltpu.SMEM)
ANY = pl.BlockSpec(memory_space=pl.ANY)
MIB = 1 << 20
NT = (((1,), (1,)), ((), ()))
NN = (((1,), (0,)), ((), ()))


def params(mib=16):
    return pltpu.CompilerParams(vmem_limit_bytes=mib * MIB)


def vmem(x):
    return pltpu.with_memory_space_constraint(x, pltpu.VMEM)


def cost(flops, nbytes):
    return pl.CostEstimate(flops=int(flops), bytes_accessed=int(nbytes), transcendentals=0)


def swap(x, axis, k=1):
    size = lax.axis_size(axis)
    return lax.ppermute(x, axis, [(i, i ^ k) for i in range(size)])


def is_pow2(size):
    return size & (size - 1) == 0


def sum_over(x, axes):
    for axis in axes:
        size = lax.axis_size(axis)
        if not is_pow2(size):
            x = lax.psum(x, axis)
        elif size == 4:
            a, b, c = swap(x, axis, 1), swap(x, axis, 2), swap(x, axis, 3)
            x = (x + a) + (b + c)
        else:
            k = 1
            while k < size:
                x = x + swap(x, axis, k)
                k *= 2
    return x


def totals_kernel(bm, nbuf, counts, compact, total, buf, sem):
    m, n = counts.shape
    steps = m // bm

    def fetch(i):
        return pltpu.make_async_copy(
            counts.at[pl.ds(i * bm, bm), :], buf.at[i % nbuf], sem.at[i % nbuf]
        )

    for i in range(min(nbuf, steps)):
        fetch(i).start()
    for i in range(steps):
        fetch(i).wait()
        slot = i % nbuf

        def tile(t, acc, slot=slot, i=i):
            at = pl.ds(pl.multiple_of(t * 128, 128), 128)
            x = buf[slot, :, at].astype(F32)
            compact[pl.ds(i * bm, bm), at] = x.astype(BF16)
            return acc + x

        acc = lax.fori_loop(0, n // 128, tile, jnp.zeros((bm, 128), F32), unroll=4)
        total[:, pl.ds(i * bm, bm)] = jnp.sum(acc.T, axis=0, keepdims=True)
        if i + nbuf < steps:
            fetch(i + nbuf).start()


def column(library, factor, m):
    for t in range(m // 128):
        row = 10000.0 / library[:, t * 128 : (t + 1) * 128]
        factor[t * 128 : (t + 1) * 128, :] = jnp.broadcast_to(row, (128, 128)).T


def logged_block(compact, factor, rows, cols, width):
    x = compact[rows, cols].astype(F32)
    s = factor[rows, :]
    s = jnp.concatenate([s] * (width // 128), axis=1)
    return jnp.log(1.0 + x * s)


def stats_kernel(compact, library, logged, stats, factor):
    m, n = compact.shape
    column(library, factor, m)
    width, bm = 512, 64

    def over_cols(t, carry):
        cols = pl.ds(pl.multiple_of(t * width, width), width)

        def over_rows(r, acc):
            rows = pl.ds(pl.multiple_of(r * bm, bm), bm)
            y = logged_block(compact, factor, rows, cols, width)
            logged[rows, cols] = y
            parts = y.reshape(bm // 8, 8, width)
            return acc[0] + jnp.sum(parts, axis=0), acc[1] + jnp.sum(parts * parts, axis=0)

        zero = jnp.zeros((8, width), F32)
        one, two = lax.fori_loop(0, m // bm, over_rows, (zero, zero))
        stats[0:1, cols] = jnp.sum(one, axis=0, keepdims=True)
        stats[1:2, cols] = jnp.sum(two, axis=0, keepdims=True)
        return carry

    lax.fori_loop(0, n // width, over_cols, 0)


def two_parts(x):
    h = x.astype(BF16)
    return h, (x - h.astype(F32)).astype(BF16)


def split_kernel(logged, high, low):
    m, n = logged.shape
    width, bm = 512, 64

    def over_rows(r, carry):
        rows = pl.ds(pl.multiple_of(r * bm, bm), bm)

        def over_cols(t, c):
            cols = pl.ds(pl.multiple_of(t * width, width), width)
            high[rows, cols], low[rows, cols] = two_parts(logged[rows, cols])
            return c

        return lax.fori_loop(0, n // width, over_cols, carry)

    lax.fori_loop(0, m // bm, over_rows, 0)


def mean_scale(stats, ncells):
    mean = stats[0:1, :] / ncells
    meansq = stats[1:2, :] / ncells
    return mean, 1.0 / jnp.sqrt(meansq - mean * mean + 1e-05)


def sketch_rows(high, low, weight, shift, at, size):
    rank = weight.shape[1] // 2
    rows = pl.ds(pl.multiple_of(at, size), size)
    acc = jnp.dot(high[rows, :], weight[...], preferred_element_type=F32)
    acc = acc + jnp.dot(low[rows, :], weight[...], preferred_element_type=F32)
    acc = acc.T
    return acc[:rank] + acc[rank:] - shift[:, 0:1]


def away_kernel(ncells, high, low, start_t, stats, away, weight, shift):
    m = high.shape[0]
    mean, scale = mean_scale(stats[...], ncells)
    w = start_t[...] * scale
    shift[...] = jnp.broadcast_to(jnp.sum(w * mean, axis=1, keepdims=True), shift.shape)
    h, l = two_parts(w)
    weight[...] = jnp.concatenate([h, l], axis=0).T
    q = m // 4
    base = (1 - lax.axis_index("sub")) * (m // 2)
    for i in range(2):
        away[i] = sketch_rows(high, low, weight, shift, base + i * q, q)


def own_kernel(i, high, low, weight, shift, own):
    m = high.shape[0]
    q = m // 4
    base = lax.axis_index("sub") * (m // 2)
    own[...] = sketch_rows(high, low, weight, shift, base + i * q, q)


def prep_kernel(own0, own1, other0, other1, sketch, packed, colsum, gram):
    rank = own0.shape[0]
    mine = jnp.concatenate([own0[...], own1[...]], axis=1)
    theirs = jnp.concatenate([other0[...], other1[...]], axis=1)
    first = lax.axis_index("sub") == 0
    s = jnp.concatenate([jnp.where(first, mine, theirs), jnp.where(first, theirs, mine)], axis=1)
    sketch[...] = s
    h, l = two_parts(s)
    packed[...] = jnp.concatenate([h, l], axis=0)
    colsum[...] = jnp.broadcast_to(jnp.sum(s, axis=1, keepdims=True), colsum.shape)
    g = lax.dot_general(s, s, NT, precision=HI, preferred_element_type=F32)
    gram[...] = jnp.concatenate([g, g], axis=1)


def eliminate(a, k0, k1):
    row = lax.broadcasted_iota(jnp.int32, (a.shape[0], 1), 0)
    for k in range(k0, k1):
        pivot = a[k : k + 1, :]
        f = a[:, k : k + 1] * (1.0 / a[k : k + 1, k : k + 1])
        a = a - jnp.where(row > k, f, 0.0) * pivot
    return a


def with_identity(gram):
    rank = gram.shape[0]
    lane = lax.broadcasted_iota(jnp.int32, (rank, 2 * rank), 1)
    row = lax.broadcasted_iota(jnp.int32, (rank, 2 * rank), 0)
    return jnp.where(lane < rank, gram, jnp.where(lane - rank == row, 1.0, 0.0))


def lower_inverse(a):
    rank = a.shape[0]
    lane = lax.broadcasted_iota(jnp.int32, (rank, rank), 1)
    row = lax.broadcasted_iota(jnp.int32, (rank, rank), 0)
    diag = jnp.sum(jnp.where(lane == row, a[:, :rank], 0.0), axis=1, keepdims=True)
    return a[:, rank:] * (1.0 / jnp.sqrt(diag))


def inverse_kernel(gram, inverse):
    rank = gram.shape[0]
    inverse[...] = lower_inverse(eliminate(with_identity(gram[...]), 0, rank))


def scores_kernel(ncells, sketch, inverse, scores):
    s = lax.dot_general(inverse[...], sketch[...], NN, precision=HI, preferred_element_type=F32)
    scores[...] = s * (float(ncells) ** 0.5)


def z_chunk(ncells, c0, nc, packed, colsum, high, low, stats):
    rank = colsum.shape[0]
    cols = slice(c0, c0 + nc)
    z = jnp.dot(packed[...], high[:, cols], preferred_element_type=F32)
    z = z + jnp.dot(packed[...], low[:, cols], preferred_element_type=F32)
    mean, scale = mean_scale(stats[:, cols], ncells)
    return (z[:rank] + z[rank:] - colsum[:, 0:1] * mean) * scale


def product_kernel(ncells, packed, colsum, high, low, stats, z):
    n = high.shape[1]
    nc = min(n, 512)
    for c0 in range(0, n, nc):
        z[:, c0 : c0 + nc] = z_chunk(ncells, c0, nc, packed, colsum, high, low, stats)


def finish_kernel(z, inverse, loadings, square):
    l = lax.dot_general(inverse[...], z[...], NN, precision=HI, preferred_element_type=F32)
    loadings[...] = l
    square[...] = lax.dot_general(l, l, NT, precision=HI, preferred_element_type=F32)


def loadings_on_a_line(ncells, sketch, packed, colsum, gram, high, low, stats):
    rank, n = colsum.shape[0], high.shape[1]
    lag, count = LAG, CHUNKS
    tiles = n // 128 + 1
    sizes = [tiles // count + (1 if i < tiles % count else 0) for i in range(count)]
    width = [128 * size for size in sizes]
    genes = [width[0] - 128] + width[1:]
    begin = [sum(genes[:i]) for i in range(count)]
    pairs = [(0, 1), (1, 0), (2, 3), (3, 2)]
    middle = [(2, 4), (4, 2), (3, 5), (5, 3), (0, 1), (1, 0), (6, 7), (7, 6)]

    slots = count + 3 * lag
    split_at = rank // 2
    finishes = {s: [] for s in range(slots)}
    ready = 3 * lag + 2
    for d in range(count):
        finishes[max(ready + d // 2, d + 3 * lag)].append(d)

    val = {}
    val["token"] = jnp.zeros((8, 128), F32)
    val["square"] = jnp.zeros((rank, rank), F32)
    val.update(packed=packed, colsum=colsum, gram=gram, stats=stats)
    val.update(high=vmem(high), low=vmem(low))

    def chunk(x):
        return jax.ShapeDtypeStruct((rank, x), F32)

    for s in range(slots):
        a, b, c = s, s - lag, s - 2 * lag
        has = lambda i: 0 <= i < count
        ins, outs = ["token"], {"token": jax.ShapeDtypeStruct((8, 128), F32)}
        if has(a):
            ins += ["packed", "colsum", "high", "low", "stats"] + (["gram"] if a == 0 else [])
            outs[f"z{a}"] = chunk(width[a])
        if has(b):
            ins += [f"z{b}", f"up{b}"]
            outs[f"s{b}"] = chunk(width[b])
        if has(c):
            ins += [f"s{c}", f"across{c}"]
            outs[f"t{c}"] = chunk(width[c])
        send = max([width[i] for i in (a, c) if has(i)], default=0)
        if send:
            outs[f"give{s}"] = chunk(send)
        if s == 3 * lag:
            ins += ["t0", "down0"]
            outs["state"] = chunk(2 * rank)
        if s == 3 * lag + 1:
            ins += ["state"]
            outs["inverse"] = chunk(rank)
        if finishes[s]:
            for d in finishes[s]:
                ins += [f"t{d}", f"down{d}"]
                outs[f"l{d}"] = chunk(genes[d])
            ins += ["inverse", "square"]
            outs["square"] = chunk(rank)
        ins = list(dict.fromkeys(ins))

        def kernel(*refs, a=a, b=b, c=c, s=s, ins=ins, names=list(outs), has=has, send=send):
            r = dict(zip(ins, refs[: len(ins)]))
            o = dict(zip(names, refs[len(ins) :]))
            z = lax.axis_index("cells")
            end = jnp.logical_or(z == 0, z == 3)
            o["token"][...] = r["token"][...]
            if has(a):
                zz = z_chunk(
                    ncells, begin[a], genes[a], r["packed"], r["colsum"], r["high"], r["low"], r["stats"]
                )
                if a == 0:
                    zz = jnp.concatenate([zz, r["gram"][...]], axis=1)
                o[f"z{a}"][...] = zz
            if has(b):
                o[f"s{b}"][...] = r[f"z{b}"][...] + r[f"up{b}"][:, : width[b]]
            if has(c):
                tt = r[f"s{c}"][...] + r[f"across{c}"][...]
                o[f"t{c}"][...] = tt
            if send:
                give = o[f"give{s}"]
                wa = width[a] if has(a) else 0
                wc = width[c] if has(c) else 0
                both = min(wa, wc)
                if both:
                    give[:, :both] = jnp.where(end, zz[:, :both], tt[:, :both])
                if wa > both:
                    give[:, both:] = zz[:, both:]
                if wc > both:
                    give[:, both:] = tt[:, both:]

            def arrived(d):
                return jnp.where(end, r[f"down{d}"][:, : width[d]], r[f"t{d}"][...])

            if s == 3 * lag:
                o["state"][...] = eliminate(with_identity(arrived(0)[:, -2 * rank :]), 0, split_at)
            if s == 3 * lag + 1:
                o["inverse"][...] = lower_inverse(eliminate(r["state"][...], split_at, rank))
            if finishes[s]:
                total = r["square"][...]
                for d in finishes[s]:
                    l = lax.dot_general(
                        r["inverse"][...],
                        arrived(d)[:, : genes[d]],
                        NN,
                        precision=HI,
                        preferred_element_type=F32,
                    )
                    o[f"l{d}"][...] = l
                    total = total + lax.dot_general(
                        l, l, NT, precision=HI, preferred_element_type=F32
                    )
                o["square"][...] = total

        results = pl.pallas_call(
            kernel,
            name=f"slot{s}",
            out_shape=tuple(outs.values()),
            in_specs=[VM] * len(ins),
            out_specs=(VM,) * len(outs),
            compiler_params=params(8),
            cost_estimate=cost(5e8, 2 * MIB),
        )(*[val[k] for k in ins])
        val.update(zip(outs, results))
        if send:
            got = lax.ppermute(val[f"give{s}"], "cells", pairs)
            if has(a):
                val[f"up{a}"] = got
            if has(c):
                val[f"down{c}"] = got
        if has(b):
            val[f"across{b}"] = lax.ppermute(val[f"s{b}"], ("cells", "sub"), middle)
    loadings = jnp.concatenate([val[f"l{d}"] for d in range(count)], axis=1)
    return loadings, val["square"], val["inverse"]


LAG, CHUNKS = 2, 6


def call(kernel, name, out_shape, args, scratch=(), mib=4, flops=0, nbytes=MIB):
    single = not isinstance(out_shape, tuple)
    return pl.pallas_call(
        kernel,
        name=name,
        out_shape=out_shape,
        in_specs=[VM] * len(args),
        out_specs=VM if single else (VM,) * len(out_shape),
        scratch_shapes=list(scratch),
        compiler_params=params(mib),
        cost_estimate=cost(flops, nbytes),
    )(*args)


def f32(*shape):
    return jax.ShapeDtypeStruct(shape, F32)


def body(counts, start_block):
    m, n = counts.shape
    rank = start_block.shape[1]
    cells = lax.axis_size("cells")
    ncells = m * cells
    genes = n * lax.axis_size("genes") * lax.axis_size("sub")

    bm, nbuf = 128, 4
    compact, total = pl.pallas_call(
        functools.partial(totals_kernel, bm, nbuf),
        name="totals",
        out_shape=(pltpu.VMEM((m, n), BF16), f32(1, m)),
        in_specs=[pl.BlockSpec(memory_space=pltpu.HBM)],
        out_specs=(VM, VM),
        scratch_shapes=[pltpu.VMEM((nbuf, bm, n), jnp.int32), pltpu.SemaphoreType.DMA((nbuf,))],
        compiler_params=params(12),
        cost_estimate=cost(0, 24 * m * n),
    )(pltpu.with_memory_space_constraint(counts, pltpu.HBM))
    library = sum_over(total, ("sub", "genes"))

    logged, stats = call(
        stats_kernel,
        "stats",
        (pltpu.VMEM((m, n), F32), f32(2, n)),
        [vmem(compact), library],
        [pltpu.VMEM((m, 128), F32)],
        nbytes=20 * m * n,
    )
    stats = sum_over(stats, ("cells",))
    high, low = call(
        split_kernel,
        "split",
        (pltpu.VMEM((m, n), BF16), pltpu.VMEM((m, n), BF16)),
        [vmem(logged)],
        nbytes=10 * m * n,
    )

    high, low = vmem(high), vmem(low)
    away, weight, shift = call(
        functools.partial(away_kernel, ncells),
        "away",
        (f32(2, rank, m // 4), jax.ShapeDtypeStruct((n, 2 * rank), BF16), f32(rank, 128)),
        [high, low, start_block.T, stats],
        flops=4 * m * n * rank,
        mib=8,
    )
    away = swap(away, "sub")
    own, other = [], []
    for i in range(2):
        part = call(
            functools.partial(own_kernel, i),
            "own",
            f32(rank, m // 4),
            [high, low, weight, shift],
            flops=2 * m * n * rank,
        )
        own.append(sum_over(part + away[i], ("genes",)))
        other.append(swap(own[i], "sub"))

    sketch, packed, colsum, gram = call(
        prep_kernel,
        "prep",
        (
            f32(rank, m),
            jax.ShapeDtypeStruct((2 * rank, m), BF16),
            f32(rank, 128),
            f32(rank, 2 * rank),
        ),
        own + other,
        flops=12 * m * rank * rank,
    )

    if cells == 4 and n % 1024 == 0 and 2 * rank == 128:
        loadings, square, inverse = loadings_on_a_line(
            ncells, sketch, packed, colsum, gram, high, low, stats
        )
    else:
        z = call(
            functools.partial(product_kernel, ncells),
            "product",
            f32(rank, n),
            [packed, colsum, high, low, stats],
            mib=8,
        )
        inverse = call(
            inverse_kernel, "inverse", f32(rank, rank), [sum_over(gram, ("cells",))]
        )
        loadings, square = call(
            finish_kernel,
            "finish",
            (f32(rank, n), f32(rank, rank)),
            [lax.psum(z, "cells"), inverse],
            mib=16,
        )

    scores = call(
        functools.partial(scores_kernel, ncells),
        "scores",
        f32(rank, m),
        [sketch, inverse],
        flops=12 * m * rank * rank,
    )
    ritz = sum_over(square, ("sub", "genes")) / genes
    return (scores.T, loadings.T, ritz)


def solution(mesh):
    placed = (P(("groups", "cells"), ("genes", "sub")), P(("genes", "sub"), None))
    return jax.shard_map(
        body,
        mesh=mesh,
        in_specs=placed,
        out_specs=(
            P(("groups", "cells"), None),
            P(("groups", "genes", "sub"), None),
            P("groups", None),
        ),
        check_vma=False,
    )
```

```python
import functools

import jax
import jax.numpy as jnp
from jax import lax
from jax.experimental import pallas as pl
from jax.experimental.pallas import tpu as pltpu
from jax.sharding import PartitionSpec as P

F32 = jnp.float32
BF16 = jnp.bfloat16
HI = lax.Precision.HIGHEST
VM = pl.BlockSpec(memory_space=pltpu.VMEM)
SM = pl.BlockSpec(memory_space=pltpu.SMEM)
ANY = pl.BlockSpec(memory_space=pl.ANY)
MIB = 1 << 20
NT = (((1,), (1,)), ((), ()))
NN = (((1,), (0,)), ((), ()))


def params(mib=16):
    return pltpu.CompilerParams(vmem_limit_bytes=mib * MIB)


def vmem(x):
    return pltpu.with_memory_space_constraint(x, pltpu.VMEM)


def cost(flops, nbytes):
    return pl.CostEstimate(flops=int(flops), bytes_accessed=int(nbytes), transcendentals=0)


def swap(x, axis, k=1):
    size = lax.axis_size(axis)
    return lax.ppermute(x, axis, [(i, i ^ k) for i in range(size)])


def is_pow2(size):
    return size & (size - 1) == 0


def sum_over(x, axes):
    for axis in axes:
        size = lax.axis_size(axis)
        if not is_pow2(size):
            x = lax.psum(x, axis)
            continue
        k = 1
        while k < size:
            x = x + swap(x, axis, k)
            k *= 2
    return x


def sum_of_four(x, axes):
    if [lax.axis_size(axis) for axis in axes] != [2, 2]:
        return sum_over(x, axes[::-1])
    a, b, c = (lax.ppermute(x, axes, [(i, i ^ k) for i in range(4)]) for k in (1, 2, 3))
    return (x + a) + (b + c)


def totals_kernel(bm, nbuf, counts, compact, total, buf, partial, sem):
    m, n = counts.shape
    steps = m // bm

    def fetch(i):
        return pltpu.make_async_copy(
            counts.at[pl.ds(i * bm, bm), :], buf.at[i % nbuf], sem.at[i % nbuf]
        )

    for i in range(min(nbuf, steps)):
        fetch(i).start()
    for i in range(steps):
        fetch(i).wait()
        slot = i % nbuf

        def tile(t, acc, slot=slot, i=i):
            at = pl.ds(pl.multiple_of(t * 128, 128), 128)
            x = buf[slot, :, at].astype(F32)
            compact[pl.ds(i * bm, bm), at] = x.astype(BF16)
            return acc + x

        acc = lax.fori_loop(0, n // 128, tile, jnp.zeros((bm, 128), F32), unroll=8)
        if i + nbuf < steps:
            fetch(i + nbuf).start()
        partial[pl.ds(i * bm, bm), :] = acc
        if (i + 1) * bm % 128 == 0:
            r = (i + 1) * bm - 128
            total[:, r : r + 128] = jnp.sum(partial[r : r + 128, :].T, axis=0, keepdims=True)


def column(library, factor, m):
    for t in range(m // 128):
        row = 10000.0 / library[:, t * 128 : (t + 1) * 128]
        factor[t * 128 : (t + 1) * 128, :] = jnp.broadcast_to(row, (128, 128)).T


def logged_block(compact, factor, rows, cols, width):
    x = compact[rows, cols].astype(F32)
    s = factor[rows, :]
    s = jnp.concatenate([s] * (width // 128), axis=1)
    return jnp.log(1.0 + x * s)


def stats_kernel(compact, library, logged, stats, factor):
    m, n = compact.shape
    column(library, factor, m)
    width, bm = 512, 64

    def over_cols(t, carry):
        cols = pl.ds(pl.multiple_of(t * width, width), width)

        def over_rows(r, acc):
            rows = pl.ds(pl.multiple_of(r * bm, bm), bm)
            y = logged_block(compact, factor, rows, cols, width)
            logged[rows, cols] = y
            parts = y.reshape(bm // 8, 8, width)
            return acc[0] + jnp.sum(parts, axis=0), acc[1] + jnp.sum(parts * parts, axis=0)

        zero = jnp.zeros((8, width), F32)
        one, two = lax.fori_loop(0, m // bm, over_rows, (zero, zero))
        stats[0:1, cols] = jnp.sum(one, axis=0, keepdims=True)
        stats[1:2, cols] = jnp.sum(two, axis=0, keepdims=True)
        return carry

    lax.fori_loop(0, n // width, over_cols, 0)


def two_parts(x):
    h = x.astype(BF16)
    return h, (x - h.astype(F32)).astype(BF16)


def split_kernel(logged, high, low):
    m, n = logged.shape
    width, bm = 512, 64

    def over_rows(r, carry):
        rows = pl.ds(pl.multiple_of(r * bm, bm), bm)

        def over_cols(t, c):
            cols = pl.ds(pl.multiple_of(t * width, width), width)
            high[rows, cols], low[rows, cols] = two_parts(logged[rows, cols])
            return c

        return lax.fori_loop(0, n // width, over_cols, carry)

    lax.fori_loop(0, m // bm, over_rows, 0)


def mean_scale(stats, ncells):
    mean = stats[0:1, :] / ncells
    meansq = stats[1:2, :] / ncells
    return mean, 1.0 / jnp.sqrt(meansq - mean * mean + 1e-05)


def sketch_rows(high, low, weight, shift, at, size):
    rank = weight.shape[1] // 2
    rows = pl.ds(pl.multiple_of(at, size), size)
    acc = jnp.dot(high[rows, :], weight[...], preferred_element_type=F32)
    acc = acc + jnp.dot(low[rows, :], weight[...], preferred_element_type=F32)
    acc = acc.T
    return acc[:rank] + acc[rank:] - shift[:, 0:1]


def away_kernel(ncells, high, low, start_t, stats, away, weight, shift):
    m = high.shape[0]
    mean, scale = mean_scale(stats[...], ncells)
    w = start_t[...] * scale
    shift[...] = jnp.broadcast_to(jnp.sum(w * mean, axis=1, keepdims=True), shift.shape)
    h, l = two_parts(w)
    weight[...] = jnp.concatenate([h, l], axis=0).T
    q = m // 4
    base = (1 - lax.axis_index("sub")) * (m // 2)
    for i in range(2):
        away[i] = sketch_rows(high, low, weight, shift, base + i * q, q)


def own_kernel(i, high, low, weight, shift, own):
    m = high.shape[0]
    q = m // 4
    base = lax.axis_index("sub") * (m // 2)
    own[...] = sketch_rows(high, low, weight, shift, base + i * q, q)


def prep_kernel(ncells, genes, *refs):
    own0, own1, other0, other1 = refs[:4]
    if genes:
        high, low, stats = refs[4:7]
    sketch, packed, colsum, gram = refs[-4:]
    rank = own0.shape[0]
    mine = jnp.concatenate([own0[...], own1[...]], axis=1)
    theirs = jnp.concatenate([other0[...], other1[...]], axis=1)
    first = lax.axis_index("sub") == 0
    s = jnp.concatenate([jnp.where(first, mine, theirs), jnp.where(first, theirs, mine)], axis=1)
    sketch[...] = s
    h, l = two_parts(s)
    packed[...] = jnp.concatenate([h, l], axis=0)
    colsum[...] = jnp.broadcast_to(jnp.sum(s, axis=1, keepdims=True), colsum.shape)
    g = lax.dot_general(s, s, NT, precision=HI, preferred_element_type=F32)
    if genes:
        gram[:, :genes] = z_chunk(ncells, 0, genes, packed, colsum, high, low, stats)
    gram[:, genes:] = jnp.concatenate([g, g], axis=1)


def eliminate(a, k0, k1):
    row = lax.broadcasted_iota(jnp.int32, (a.shape[0], 1), 0)
    for k in range(k0, k1):
        pivot = a[k : k + 1, :]
        f = a[:, k : k + 1] * (1.0 / a[k : k + 1, k : k + 1])
        a = a - jnp.where(row > k, f, 0.0) * pivot
    return a


def with_identity(gram):
    rank = gram.shape[0]
    lane = lax.broadcasted_iota(jnp.int32, (rank, 2 * rank), 1)
    row = lax.broadcasted_iota(jnp.int32, (rank, 2 * rank), 0)
    return jnp.where(lane < rank, gram, jnp.where(lane - rank == row, 1.0, 0.0))


def lower_inverse(a):
    rank = a.shape[0]
    lane = lax.broadcasted_iota(jnp.int32, (rank, rank), 1)
    row = lax.broadcasted_iota(jnp.int32, (rank, rank), 0)
    diag = jnp.sum(jnp.where(lane == row, a[:, :rank], 0.0), axis=1, keepdims=True)
    return a[:, rank:] * (1.0 / jnp.sqrt(diag))


def inverse_kernel(gram, inverse):
    rank = gram.shape[0]
    inverse[...] = lower_inverse(eliminate(with_identity(gram[...]), 0, rank))


def dot_hi(x, y, dims):
    return lax.dot_general(x, y, dims, precision=HI, preferred_element_type=F32)


def scores_kernel(ncells, sketch, inverse, scores):
    s = lax.dot_general(inverse[...], sketch[...], NN, precision=HI, preferred_element_type=F32)
    scores[...] = s * (float(ncells) ** 0.5)


def z_chunk(ncells, c0, nc, packed, colsum, high, low, stats):
    rank = colsum.shape[0]
    cols = slice(c0, c0 + nc)
    z = jnp.dot(packed[...], high[:, cols], preferred_element_type=F32)
    z = z + jnp.dot(packed[...], low[:, cols], preferred_element_type=F32)
    mean, scale = mean_scale(stats[:, cols], ncells)
    return (z[:rank] + z[rank:] - colsum[:, 0:1] * mean) * scale


def product_kernel(ncells, packed, colsum, high, low, stats, z):
    n = high.shape[1]
    nc = min(n, 512)
    for c0 in range(0, n, nc):
        z[:, c0 : c0 + nc] = z_chunk(ncells, c0, nc, packed, colsum, high, low, stats)


def finish_kernel(z, inverse, loadings, square):
    l = lax.dot_general(inverse[...], z[...], NN, precision=HI, preferred_element_type=F32)
    loadings[...] = l
    square[...] = lax.dot_general(l, l, NT, precision=HI, preferred_element_type=F32)


def layout(n):
    count = CHUNKS
    tiles = n // 128 + 1
    sizes = [128 * (tiles // count + (1 if i < tiles % count else 0)) for i in range(count)]
    return [sizes[0] - 128] + sizes[1:]


def loadings_on_a_line(ncells, sketch, packed, colsum, first, high, low, stats):
    rank, n, m = colsum.shape[0], high.shape[1], sketch.shape[1]
    lag, count = LAG, CHUNKS
    genes = layout(n)
    width = [genes[0] + 2 * rank] + genes[1:]
    begin = [sum(genes[:i]) for i in range(count)]
    pairs = [(0, 1), (1, 0), (2, 3), (3, 2)]
    middle = [(2, 4), (4, 2), (3, 5), (5, 3), (0, 1), (1, 0), (6, 7), (7, 6)]

    slots = count + 3 * lag
    parts = 4
    step = rank // parts
    back = 3 * lag
    finishes, queue = {}, []
    for s in range(slots):
        queue += [s - back] if 0 <= s - back < count else []
        take = 0 if s < back + parts else 3
        finishes[s], queue = queue[:take], queue[take:]

    def chunk(x):
        return jax.ShapeDtypeStruct((rank, x), F32)

    def has(i):
        return 0 <= i < count

    def run(name, ins, outs, kernel):
        def wrapped(*refs):
            kernel(dict(zip(ins, refs)), dict(zip(outs, refs[len(ins) :])))

        results = pl.pallas_call(
            wrapped,
            name=name,
            out_shape=tuple(outs.values()),
            in_specs=[VM] * len(ins),
            out_specs=(VM,) * len(outs),
            compiler_params=params(8),
            cost_estimate=cost(1e6, 1 << 16),
        )(*[val[k] for k in ins])
        val.update(zip(outs, results))

    def at_end():
        z = lax.axis_index("cells")
        return jnp.logical_or(z == 0, z == 3)

    def arrived(d, r):
        return jnp.where(at_end(), r[f"down{d}"][:, : width[d]], r[f"t{d}"][...])

    token = jax.ShapeDtypeStruct((8, 128), F32)
    val = dict(token=jnp.zeros((8, 128), F32), square=jnp.zeros((rank, rank), F32))
    val.update(packed=packed, colsum=colsum, stats=stats, z0=first, sketch=sketch)
    val.update(high=vmem(high), low=vmem(low))

    def main_slot(s, a, b, c):
        ins, outs = ["token"], {"token": token}
        if has(a):
            ins += [f"z{a}"]
        if has(b):
            ins += [f"z{b}", f"up{b}"]
            outs[f"s{b}"] = chunk(width[b])
        if has(c):
            ins += [f"s{c}", f"across{c}"]
            outs[f"t{c}"] = chunk(width[c])
        send = max([width[i] for i in (a, c) if has(i)], default=0)
        if has(a) and has(c):
            outs[f"give{s}"] = chunk(send)

        def kernel(r, o):
            o["token"][...] = r["token"][...]
            if has(b):
                o[f"s{b}"][...] = r[f"z{b}"][...] + r[f"up{b}"][:, : width[b]]
            if has(c):
                tt = r[f"s{c}"][...] + r[f"across{c}"][...]
                o[f"t{c}"][...] = tt
            if has(a) and has(c):
                zz, give = r[f"z{a}"], o[f"give{s}"]
                both = min(width[a], width[c])
                give[:, :both] = jnp.where(at_end(), zz[:, :both], tt[:, :both])
                if width[a] > both:
                    give[:, both:] = zz[:, both:]
                if width[c] > both:
                    give[:, both:] = tt[:, both:]

        if has(b) or has(c):
            run(f"slot{s}", ins, outs, kernel)
        if has(a) and has(c):
            return val[f"give{s}"]
        return val[f"z{a}"] if has(a) else val[f"t{c}"] if has(c) else None

    def side_slot(s, a):
        ins, outs = ["token"], {"token": token}
        part = s - back
        if has(a):
            ins += ["packed", "colsum", "high", "low", "stats"]
            outs[f"z{a}"] = chunk(width[a])
        if 0 <= part < parts:
            ins += ["t0", "down0"] if part == 0 else ["state"]
            if part == parts - 1:
                outs["inverse"] = chunk(rank)
            else:
                outs["state"] = chunk(2 * rank)
        if finishes[s]:
            for d in finishes[s]:
                ins += [f"t{d}", f"down{d}"]
                outs[f"l{d}"] = chunk(genes[d])
            ins += ["inverse", "square"]
            outs["square"] = chunk(rank)
        scores = s == slots - 2
        if scores:
            ins += ["sketch", "inverse"]
            outs["scores"] = chunk(m)
        ins = list(dict.fromkeys(ins))

        def kernel(r, o):
            o["token"][...] = r["token"][...]
            if has(a):
                o[f"z{a}"][...] = z_chunk(
                    ncells, begin[a], genes[a], r["packed"], r["colsum"], r["high"], r["low"], r["stats"]
                )
            if 0 <= part < parts:
                if part == 0:
                    x = with_identity(arrived(0, r)[:, -2 * rank :])
                else:
                    x = r["state"][...]
                x = eliminate(x, part * step, (part + 1) * step)
                if part == parts - 1:
                    o["inverse"][...] = lower_inverse(x)
                else:
                    o["state"][...] = x
            if finishes[s]:
                total = r["square"][...]
                for d in finishes[s]:
                    l = dot_hi(r["inverse"][...], arrived(d, r)[:, : genes[d]], NN)
                    o[f"l{d}"][...] = l
                    total = total + dot_hi(l, l, NT)
                o["square"][...] = total
            if scores:
                o["scores"][...] = dot_hi(r["inverse"][...], r["sketch"][...], NN) * (
                    float(ncells) ** 0.5
                )

        if len(outs) > 1:
            run(f"side{s}", ins, outs, kernel)

    for s in range(slots):
        a, b, c = s, s - lag, s - 2 * lag
        give = main_slot(s, a, b, c)
        if give is not None:
            got = lax.ppermute(give, "cells", pairs)
            if has(a):
                val[f"up{a}"] = got
            if has(c):
                val[f"down{c}"] = got
        if has(b):
            val[f"across{b}"] = lax.ppermute(val[f"s{b}"], ("cells", "sub"), middle)
        side_slot(s, a + 1)
    loadings = jnp.concatenate([val[f"l{d}"] for d in range(count)], axis=1)
    return loadings, val["square"], val["scores"]


LAG, CHUNKS = 2, 8


def call(kernel, name, out_shape, args, scratch=(), mib=4, flops=0, nbytes=MIB):
    single = not isinstance(out_shape, tuple)
    return pl.pallas_call(
        kernel,
        name=name,
        out_shape=out_shape,
        in_specs=[VM] * len(args),
        out_specs=VM if single else (VM,) * len(out_shape),
        scratch_shapes=list(scratch),
        compiler_params=params(mib),
        cost_estimate=cost(flops, nbytes),
    )(*args)


def f32(*shape):
    return jax.ShapeDtypeStruct(shape, F32)


def body(counts, start_block):
    m, n = counts.shape
    rank = start_block.shape[1]
    cells = lax.axis_size("cells")
    ncells = m * cells
    genes = n * lax.axis_size("genes") * lax.axis_size("sub")

    bm, nbuf = 64, 8
    compact, total = pl.pallas_call(
        functools.partial(totals_kernel, bm, nbuf),
        name="totals",
        out_shape=(pltpu.VMEM((m, n), BF16), f32(1, m)),
        in_specs=[pl.BlockSpec(memory_space=pltpu.HBM)],
        out_specs=(VM, VM),
        scratch_shapes=[
            pltpu.VMEM((nbuf, bm, n), jnp.int32),
            pltpu.VMEM((m, 128), F32),
            pltpu.SemaphoreType.DMA((nbuf,)),
        ],
        compiler_params=params(12),
        cost_estimate=cost(0, 24 * m * n),
    )(pltpu.with_memory_space_constraint(counts, pltpu.HBM))
    library = sum_over(total, ("sub", "genes"))

    logged, stats = call(
        stats_kernel,
        "stats",
        (pltpu.VMEM((m, n), F32), f32(2, n)),
        [vmem(compact), library],
        [pltpu.VMEM((m, 128), F32)],
        nbytes=20 * m * n,
    )
    stats = sum_over(stats, ("cells",))
    high, low = call(
        split_kernel,
        "split",
        (pltpu.VMEM((m, n), BF16), pltpu.VMEM((m, n), BF16)),
        [vmem(logged)],
        nbytes=10 * m * n,
    )

    high, low = vmem(high), vmem(low)
    away, weight, shift = call(
        functools.partial(away_kernel, ncells),
        "away",
        (f32(2, rank, m // 4), jax.ShapeDtypeStruct((n, 2 * rank), BF16), f32(rank, 128)),
        [high, low, start_block.T, stats],
        flops=4 * m * n * rank,
        mib=8,
    )
    away = swap(away, "sub")
    own, other = [], []
    for i in range(2):
        part = call(
            functools.partial(own_kernel, i),
            "own",
            f32(rank, m // 4),
            [high, low, weight, shift],
            flops=2 * m * n * rank,
        )
        own.append(sum_over(part + away[i], ("genes",)))
        other.append(swap(own[i], "sub"))

    line = cells == 4 and n % 1024 == 0 and 2 * rank == 128
    genes0 = layout(n)[0] if line else 0
    sketch, packed, colsum, gram = call(
        functools.partial(prep_kernel, ncells, genes0),
        "prep",
        (
            f32(rank, m),
            jax.ShapeDtypeStruct((2 * rank, m), BF16),
            f32(rank, 128),
            f32(rank, genes0 + 2 * rank),
        ),
        own + other + ([high, low, stats] if line else []),
        flops=12 * m * rank * rank,
        mib=8,
    )

    if line:
        loadings, square, scores = loadings_on_a_line(
            ncells, sketch, packed, colsum, gram, high, low, stats
        )
    else:
        z = call(
            functools.partial(product_kernel, ncells),
            "product",
            f32(rank, n),
            [packed, colsum, high, low, stats],
            mib=8,
        )
        inverse = call(
            inverse_kernel, "inverse", f32(rank, rank), [sum_over(gram, ("cells",))]
        )
        loadings, square = call(
            finish_kernel,
            "finish",
            (f32(rank, n), f32(rank, rank)),
            [lax.psum(z, "cells"), inverse],
            mib=16,
        )
        scores = call(
            functools.partial(scores_kernel, ncells), "scores", f32(rank, m), [sketch, inverse]
        )
    ritz = sum_of_four(square, ("genes", "sub")) / genes
    return (scores.T, loadings.T, ritz)


def solution(mesh):
    placed = (P(("groups", "cells"), ("genes", "sub")), P(("genes", "sub"), None))
    return jax.shard_map(
        body,
        mesh=mesh,
        in_specs=placed,
        out_specs=(
            P(("groups", "cells"), None),
            P(("groups", "genes", "sub"), None),
            P("groups", None),
        ),
        check_vma=False,
    )
```

```python
import functools

import jax
import jax.numpy as jnp
from jax import lax
from jax.experimental import pallas as pl
from jax.experimental.pallas import tpu as pltpu
from jax.sharding import PartitionSpec as P

F32 = jnp.float32
BF16 = jnp.bfloat16
HI = lax.Precision.HIGHEST
VM = pl.BlockSpec(memory_space=pltpu.VMEM)
SM = pl.BlockSpec(memory_space=pltpu.SMEM)
ANY = pl.BlockSpec(memory_space=pl.ANY)
MIB = 1 << 20
LN2 = 0.6931471805599453
NT = (((1,), (1,)), ((), ()))
NN = (((1,), (0,)), ((), ()))


def params(mib=16):
    return pltpu.CompilerParams(vmem_limit_bytes=mib * MIB)


def vmem(x):
    return pltpu.with_memory_space_constraint(x, pltpu.VMEM)


def cost(flops, nbytes):
    return pl.CostEstimate(flops=int(flops), bytes_accessed=int(nbytes), transcendentals=0)


def swap(x, axis, k=1):
    size = lax.axis_size(axis)
    return lax.ppermute(x, axis, [(i, i ^ k) for i in range(size)])


def is_pow2(size):
    return size & (size - 1) == 0


def sum_over(x, axes):
    for axis in axes:
        size = lax.axis_size(axis)
        if not is_pow2(size):
            x = lax.psum(x, axis)
            continue
        k = 1
        while k < size:
            x = x + swap(x, axis, k)
            k *= 2
    return x


def sum_of_four(x, axes):
    if [lax.axis_size(axis) for axis in axes] != [2, 2]:
        return sum_over(x, axes[::-1])
    a, b, c = (lax.ppermute(x, axes, [(i, i ^ k) for i in range(4)]) for k in (1, 2, 3))
    return (x + a) + (b + c)


def totals_kernel(bm, counts, held, total, sem):
    m, n = counts.shape

    def fetch(i):
        rows = pl.ds(i * bm, bm)
        return pltpu.make_async_copy(counts.at[rows, :], held.at[rows, :], sem.at[i])

    for i in range(m // bm):
        fetch(i).start()
    for i in range(m // bm):
        fetch(i).wait()

        def tile(t, acc, i=i):
            return acc + held[pl.ds(i * bm, bm), pl.ds(pl.multiple_of(t * 128, 128), 128)]

        acc = lax.fori_loop(0, n // 128, tile, jnp.zeros((bm, 128), jnp.int32), unroll=8)
        acc = acc.astype(F32)
        for r in range(0, bm, 128):
            row = jnp.sum(acc[r : r + 128].T, axis=0, keepdims=True)
            total[:, i * bm + r : i * bm + r + 128] = row


def column(library, factor, m):
    for t in range(m // 128):
        row = 10000.0 / library[:, t * 128 : (t + 1) * 128]
        factor[t * 128 : (t + 1) * 128, :] = jnp.broadcast_to(row, (128, 128)).T


def stats_kernel(held, library, logged, stats, factor):
    m, n = held.shape
    column(library, factor, m)
    width, bm = 512, 64

    def over_cols(t, carry):
        cols = pl.ds(pl.multiple_of(t * width, width), width)

        def over_rows(r, acc):
            rows = pl.ds(pl.multiple_of(r * bm, bm), bm)
            s = factor[rows, :]
            s = jnp.concatenate([s] * (width // 128), axis=1)
            y = jnp.log2(1.0 + held[rows, cols].astype(F32) * s)
            logged[rows, cols] = y
            parts = y.reshape(bm // 8, 8, width)
            return acc[0] + jnp.sum(parts, axis=0), acc[1] + jnp.sum(parts * parts, axis=0)

        zero = jnp.zeros((8, width), F32)
        one, two = lax.fori_loop(0, m // bm, over_rows, (zero, zero))
        stats[0:1, cols] = jnp.sum(one, axis=0, keepdims=True)
        stats[1:2, cols] = jnp.sum(two, axis=0, keepdims=True)
        return carry

    lax.fori_loop(0, n // width, over_cols, 0)


def two_parts(x):
    h = x.astype(BF16)
    return h, (x - h.astype(F32)).astype(BF16)


def split_kernel(begin, logged, high, low):
    m, n = high.shape
    width, bm = 512, 64

    def over_rows(r, carry):
        rows = pl.ds(pl.multiple_of(r * bm, bm), bm)
        source = pl.ds(pl.multiple_of(begin + r * bm, bm), bm)

        def over_cols(t, c):
            cols = pl.ds(pl.multiple_of(t * width, width), width)
            high[rows, cols], low[rows, cols] = two_parts(logged[source, cols])
            return c

        return lax.fori_loop(0, n // width, over_cols, carry)

    lax.fori_loop(0, m // bm, over_rows, 0)


def mean_scale(stats, ncells):
    mean = stats[0:1, :] / ncells
    meansq = stats[1:2, :] / ncells
    return mean, LN2 / jnp.sqrt((LN2 * LN2) * (meansq - mean * mean) + 1e-05)


def sketch_rows(high, low, weight, shift, at, size):
    rank = weight.shape[1] // 2
    rows = slice(at, at + size)
    acc = jnp.dot(high[rows, :], weight[...], preferred_element_type=F32)
    acc = acc + jnp.dot(low[rows, :], weight[...], preferred_element_type=F32)
    acc = acc.T
    return acc[:rank] + acc[rank:] - shift[:, 0:1]


def away_kernel(ncells, high0, low0, high1, low1, start_t, stats, away, weight, shift):
    q = high0.shape[0] // 2
    mean, scale = mean_scale(stats[...], ncells)
    w = start_t[...] * scale
    shift[...] = jnp.broadcast_to(jnp.sum(w * mean, axis=1, keepdims=True), shift.shape)
    h, l = two_parts(w)
    weight[...] = jnp.concatenate([h, l], axis=0).T
    me = lax.axis_index("sub")

    def half(high, low):
        for i in range(2):
            away[i] = sketch_rows(high, low, weight, shift, i * q, q)

    pl.when(me == 1)(lambda: half(high0, low0))
    pl.when(me == 0)(lambda: half(high1, low1))


def own_kernel(i, high0, low0, high1, low1, weight, shift, own):
    q = high0.shape[0] // 2
    me = lax.axis_index("sub")

    def half(high, low):
        own[...] = sketch_rows(high, low, weight, shift, i * q, q)

    pl.when(me == 0)(lambda: half(high0, low0))
    pl.when(me == 1)(lambda: half(high1, low1))


def prep_kernel(ncells, genes, *refs):
    own0, own1, other0, other1 = refs[:4]
    if genes:
        halves, stats = refs[4:8], refs[8]
    sketch, packed, colsum, gram = refs[-4:]
    rank = own0.shape[0]
    mine = jnp.concatenate([own0[...], own1[...]], axis=1)
    theirs = jnp.concatenate([other0[...], other1[...]], axis=1)
    first = lax.axis_index("sub") == 0
    s = jnp.concatenate([jnp.where(first, mine, theirs), jnp.where(first, theirs, mine)], axis=1)
    sketch[...] = s
    h, l = two_parts(s)
    packed[...] = jnp.concatenate([h, l], axis=0)
    colsum[...] = jnp.broadcast_to(jnp.sum(s, axis=1, keepdims=True), colsum.shape)
    g = lax.dot_general(s, s, NT, precision=HI, preferred_element_type=F32)
    if genes:
        gram[:, :genes] = z_chunk(ncells, 0, genes, packed, colsum, halves, stats)
    gram[:, genes:] = jnp.concatenate([g, g], axis=1)


def eliminate(a, k0, k1):
    row = lax.broadcasted_iota(jnp.int32, (a.shape[0], 1), 0)
    for k in range(k0, k1):
        pivot = a[k : k + 1, :]
        f = a[:, k : k + 1] * (1.0 / a[k : k + 1, k : k + 1])
        a = a - jnp.where(row > k, f, 0.0) * pivot
    return a


def with_identity(gram):
    rank = gram.shape[0]
    lane = lax.broadcasted_iota(jnp.int32, (rank, 2 * rank), 1)
    row = lax.broadcasted_iota(jnp.int32, (rank, 2 * rank), 0)
    return jnp.where(lane < rank, gram, jnp.where(lane - rank == row, 1.0, 0.0))


def lower_inverse(a):
    rank = a.shape[0]
    lane = lax.broadcasted_iota(jnp.int32, (rank, rank), 1)
    row = lax.broadcasted_iota(jnp.int32, (rank, rank), 0)
    diag = jnp.sum(jnp.where(lane == row, a[:, :rank], 0.0), axis=1, keepdims=True)
    return a[:, rank:] * (1.0 / jnp.sqrt(diag))


def inverse_kernel(gram, inverse):
    rank = gram.shape[0]
    inverse[...] = lower_inverse(eliminate(with_identity(gram[...]), 0, rank))


def dot_hi(x, y, dims):
    return lax.dot_general(x, y, dims, precision=HI, preferred_element_type=F32)


def scores_kernel(ncells, sketch, inverse, scores):
    s = lax.dot_general(inverse[...], sketch[...], NN, precision=HI, preferred_element_type=F32)
    scores[...] = s * (float(ncells) ** 0.5)


def z_chunk(ncells, c0, nc, packed, colsum, halves, stats):
    rank = colsum.shape[0]
    half = packed.shape[1] // 2
    cols = slice(c0, c0 + nc)
    z = None
    for i, part in enumerate(halves):
        at = (i // 2) * half
        d = jnp.dot(packed[:, at : at + half], part[:, cols], preferred_element_type=F32)
        z = d if z is None else z + d
    mean, scale = mean_scale(stats[:, cols], ncells)
    return (z[:rank] + z[rank:] - colsum[:, 0:1] * mean) * scale


def product_kernel(ncells, packed, colsum, high0, low0, high1, low1, stats, z):
    n = high0.shape[1]
    nc = min(n, 512)
    halves = (high0, low0, high1, low1)
    for c0 in range(0, n, nc):
        z[:, c0 : c0 + nc] = z_chunk(ncells, c0, nc, packed, colsum, halves, stats)


def dot_parts(x, y, dims):
    xh, xl = two_parts(x)
    yh, yl = two_parts(y)

    def dot(a, b):
        return lax.dot_general(a, b, dims, preferred_element_type=F32)

    return dot(xh, yh) + (dot(xh, yl) + dot(xl, yh))


def finish_kernel(z, inverse, loadings, square):
    l = dot_parts(inverse[...], z[...], NN)
    loadings[...] = l
    square[...] = dot_parts(l, l, NT)


def layout(n):
    tiles = n // 128 + 1
    share = [s * tiles / sum(SHARES) for s in SHARES]
    edges = [round(sum(share[:i])) for i in range(len(share) + 1)]
    sizes = [128 * (b - a) for a, b in zip(edges, edges[1:])]
    return [sizes[0] - 128] + sizes[1:]


def loadings_on_a_line(ncells, sketch, packed, colsum, first, halves, stats):
    rank, n, m = colsum.shape[0], stats.shape[1], sketch.shape[1]
    lag, count = LAG, len(SHARES)
    genes = layout(n)
    width = [genes[0] + 2 * rank] + genes[1:]
    begin = [sum(genes[:i]) for i in range(count)]
    pairs = [(0, 1), (1, 0), (2, 3), (3, 2)]
    middle = [(2, 4), (4, 2), (3, 5), (5, 3), (0, 1), (1, 0), (6, 7), (7, 6)]

    slots = count + 3 * lag
    parts = 4
    step = rank // parts
    back = 3 * lag
    finishes, queue = {}, []
    for s in range(slots):
        queue += [s - back] if 0 <= s - back < count else []
        take = 0 if s < back + parts else 3
        finishes[s], queue = queue[:take], queue[take:]

    def chunk(x):
        return jax.ShapeDtypeStruct((rank, x), F32)

    def has(i):
        return 0 <= i < count

    def run(name, ins, outs, kernel):
        def wrapped(*refs):
            kernel(dict(zip(ins, refs)), dict(zip(outs, refs[len(ins) :])))

        results = pl.pallas_call(
            wrapped,
            name=name,
            out_shape=tuple(outs.values()),
            in_specs=[VM] * len(ins),
            out_specs=(VM,) * len(outs),
            compiler_params=params(8),
            cost_estimate=cost(1e6, 1 << 16),
        )(*[val[k] for k in ins])
        val.update(zip(outs, results))

    def at_end():
        z = lax.axis_index("cells")
        return jnp.logical_or(z == 0, z == 3)

    def arrived(d, r):
        return jnp.where(at_end(), r[f"down{d}"][:, : width[d]], r[f"t{d}"][...])

    token = jax.ShapeDtypeStruct((8, 128), F32)
    val = dict(token=jnp.zeros((8, 128), F32), square=jnp.zeros((rank, rank), F32))
    val.update(packed=packed, colsum=colsum, stats=stats, z0=first, sketch=sketch)
    val.update(zip(PARTS, halves))

    def main_slot(s, a, b, c):
        ins, outs = ["token"], {"token": token}
        if has(a):
            ins += [f"z{a}"]
        if has(b):
            ins += [f"z{b}", f"up{b}"]
            outs[f"s{b}"] = chunk(width[b])
        if has(c):
            ins += [f"s{c}", f"across{c}"]
            outs[f"t{c}"] = chunk(width[c])
        send = max([width[i] for i in (a, c) if has(i)], default=0)
        if has(a) and has(c):
            outs[f"give{s}"] = chunk(send)

        def kernel(r, o):
            o["token"][...] = r["token"][...]
            if has(b):
                o[f"s{b}"][...] = r[f"z{b}"][...] + r[f"up{b}"][:, : width[b]]
            if has(c):
                tt = r[f"s{c}"][...] + r[f"across{c}"][...]
                o[f"t{c}"][...] = tt
            if has(a) and has(c):
                zz, give = r[f"z{a}"], o[f"give{s}"]
                both = min(width[a], width[c])
                give[:, :both] = jnp.where(at_end(), zz[:, :both], tt[:, :both])
                if width[a] > both:
                    give[:, both:] = zz[:, both:]
                if width[c] > both:
                    give[:, both:] = tt[:, both:]

        if has(b) or has(c):
            run(f"slot{s}", ins, outs, kernel)
        if has(a) and has(c):
            return val[f"give{s}"]
        return val[f"z{a}"] if has(a) else val[f"t{c}"] if has(c) else None

    def side_slot(s, a):
        ins, outs = ["token"], {"token": token}
        part = s - back
        if has(a):
            ins += ["packed", "colsum", "stats", *PARTS]
            outs[f"z{a}"] = chunk(width[a])
        if 0 <= part < parts:
            ins += ["t0", "down0"] if part == 0 else ["state"]
            if part == parts - 1:
                outs["inverse"] = chunk(rank)
            else:
                outs["state"] = chunk(2 * rank)
        if finishes[s]:
            for d in finishes[s]:
                ins += [f"t{d}", f"down{d}"]
                outs[f"l{d}"] = chunk(genes[d])
            ins += ["inverse", "square"]
            outs["square"] = chunk(rank)
        ins = list(dict.fromkeys(ins))

        def kernel(r, o):
            o["token"][...] = r["token"][...]
            if has(a):
                o[f"z{a}"][...] = z_chunk(
                    ncells,
                    begin[a],
                    genes[a],
                    r["packed"],
                    r["colsum"],
                    [r[k] for k in PARTS],
                    r["stats"],
                )
            if 0 <= part < parts:
                if part == 0:
                    x = with_identity(arrived(0, r)[:, -2 * rank :])
                else:
                    x = r["state"][...]
                x = eliminate(x, part * step, (part + 1) * step)
                if part == parts - 1:
                    o["inverse"][...] = lower_inverse(x)
                else:
                    o["state"][...] = x
            if finishes[s]:
                total = r["square"][...]
                for d in finishes[s]:
                    l = dot_parts(r["inverse"][...], arrived(d, r)[:, : genes[d]], NN)
                    o[f"l{d}"][...] = l
                    total = total + dot_parts(l, l, NT)
                o["square"][...] = total

        if len(outs) > 1:
            run(f"side{s}", ins, outs, kernel)

    for s in range(slots):
        a, b, c = s, s - lag, s - 2 * lag
        give = main_slot(s, a, b, c)
        if give is not None:
            got = lax.ppermute(give, "cells", pairs)
            if has(a):
                val[f"up{a}"] = got
            if has(c):
                val[f"down{c}"] = got
        if has(b):
            val[f"across{b}"] = lax.ppermute(val[f"s{b}"], ("cells", "sub"), middle)
        side_slot(s, a + 1)

    def last(r, o):
        o["scores"][...] = dot_parts(r["inverse"][...], r["sketch"][...], NN) * (
            float(ncells) ** 0.5
        )
        for d in range(count):
            o["loadings"][:, begin[d] : begin[d] + genes[d]] = r[f"l{d}"][...]

    pieces = [f"l{d}" for d in range(count)]
    run("last", ["token", "inverse", "sketch"] + pieces, dict(scores=chunk(m), loadings=chunk(n)), last)
    return val["loadings"], val["square"], val["scores"]


PARTS = ("high0", "low0", "high1", "low1")
LAG, SHARES = 2, (3, 4, 5, 5, 5, 5, 4, 2)


def call(kernel, name, out_shape, args, scratch=(), mib=4, flops=0, nbytes=MIB):
    single = not isinstance(out_shape, tuple)
    return pl.pallas_call(
        kernel,
        name=name,
        out_shape=out_shape,
        in_specs=[VM] * len(args),
        out_specs=VM if single else (VM,) * len(out_shape),
        scratch_shapes=list(scratch),
        compiler_params=params(mib),
        cost_estimate=cost(flops, nbytes),
    )(*args)


def f32(*shape):
    return jax.ShapeDtypeStruct(shape, F32)


def body(counts, start_block):
    m, n = counts.shape
    rank = start_block.shape[1]
    cells = lax.axis_size("cells")
    ncells = m * cells
    genes = n * lax.axis_size("genes") * lax.axis_size("sub")

    bm = 128
    held, total = pl.pallas_call(
        functools.partial(totals_kernel, bm),
        name="totals",
        out_shape=(pltpu.VMEM((m, n), jnp.int32), f32(1, m)),
        in_specs=[pl.BlockSpec(memory_space=pltpu.HBM)],
        out_specs=(VM, VM),
        scratch_shapes=[pltpu.SemaphoreType.DMA((m // bm,))],
        compiler_params=params(4),
        cost_estimate=cost(0, 24 * m * n),
    )(pltpu.with_memory_space_constraint(counts, pltpu.HBM))
    library = sum_over(total, ("sub", "genes"))

    logged, stats = call(
        stats_kernel,
        "stats",
        (pltpu.VMEM((m, n), F32), f32(2, n)),
        [vmem(held), library],
        [pltpu.VMEM((m, 128), F32)],
        nbytes=20 * m * n,
    )
    logged = vmem(logged)

    def split(i, logged):
        return call(
            functools.partial(split_kernel, i * (m // 2)),
            "split",
            (pltpu.VMEM((m // 2, n), BF16), pltpu.VMEM((m // 2, n), BF16)),
            [logged],
            nbytes=4 * m * n,
        )

    halves = [split(0, logged)]
    size = cells if is_pow2(cells) else 1
    if size == 1:
        stats = lax.psum(stats, "cells")
    k = 1
    while k < size:
        got = swap(stats, "cells", k)
        if k == 1:
            got, *halves[0] = lax.optimization_barrier((got, *halves[0]))
        stats = stats + got
        k *= 2
    halves = [*halves[0], *split(1, logged)]

    halves = [vmem(x) for x in halves]
    away, weight, shift = call(
        functools.partial(away_kernel, ncells),
        "away",
        (f32(2, rank, m // 4), jax.ShapeDtypeStruct((n, 2 * rank), BF16), f32(rank, 128)),
        [*halves, start_block.T, stats],
        flops=4 * m * n * rank,
        mib=8,
    )
    away = swap(away, "sub")
    own, other = [], []
    for i in range(2):
        part = call(
            functools.partial(own_kernel, i),
            "own",
            f32(rank, m // 4),
            [*halves, weight, shift],
            flops=2 * m * n * rank,
        )
        own.append(sum_over(part + away[i], ("genes",)))
        other.append(swap(own[i], "sub"))

    line = cells == 4 and n % 1024 == 0 and 2 * rank == 128
    genes0 = layout(n)[0] if line else 0
    sketch, packed, colsum, gram = call(
        functools.partial(prep_kernel, ncells, genes0),
        "prep",
        (
            f32(rank, m),
            jax.ShapeDtypeStruct((2 * rank, m), BF16),
            f32(rank, 128),
            f32(rank, genes0 + 2 * rank),
        ),
        own + other + ([*halves, stats] if line else []),
        flops=12 * m * rank * rank,
        mib=8,
    )

    if line:
        loadings, square, scores = loadings_on_a_line(
            ncells, sketch, packed, colsum, gram, halves, stats
        )
    else:
        z = call(
            functools.partial(product_kernel, ncells),
            "product",
            f32(rank, n),
            [packed, colsum, *halves, stats],
            mib=8,
        )
        inverse = call(
            inverse_kernel, "inverse", f32(rank, rank), [sum_over(gram, ("cells",))]
        )
        loadings, square = call(
            finish_kernel,
            "finish",
            (f32(rank, n), f32(rank, rank)),
            [lax.psum(z, "cells"), inverse],
            mib=16,
        )
        scores = call(
            functools.partial(scores_kernel, ncells), "scores", f32(rank, m), [sketch, inverse]
        )
    ritz = sum_of_four(square, ("genes", "sub")) / genes
    return (scores.T, loadings.T, ritz)


def solution(mesh):
    placed = (P(("groups", "cells"), ("genes", "sub")), P(("genes", "sub"), None))
    return jax.shard_map(
        body,
        mesh=mesh,
        in_specs=placed,
        out_specs=(
            P(("groups", "cells"), None),
            P(("groups", "genes", "sub"), None),
            P("groups", None),
        ),
        check_vma=False,
    )
```

```python
import functools

import jax
import jax.numpy as jnp
from jax import lax
from jax.experimental import pallas as pl
from jax.experimental.pallas import tpu as pltpu
from jax.sharding import PartitionSpec as P

F32 = jnp.float32
BF16 = jnp.bfloat16
HI = lax.Precision.HIGHEST
VM = pl.BlockSpec(memory_space=pltpu.VMEM)
SM = pl.BlockSpec(memory_space=pltpu.SMEM)
ANY = pl.BlockSpec(memory_space=pl.ANY)
MIB = 1 << 20
LN2 = 0.6931471805599453
NT = (((1,), (1,)), ((), ()))
NN = (((1,), (0,)), ((), ()))


def params(mib=16):
    return pltpu.CompilerParams(vmem_limit_bytes=mib * MIB)


def vmem(x):
    return pltpu.with_memory_space_constraint(x, pltpu.VMEM)


def cost(flops, nbytes):
    return pl.CostEstimate(flops=int(flops), bytes_accessed=int(nbytes), transcendentals=0)


def swap(x, axis, k=1):
    size = lax.axis_size(axis)
    return lax.ppermute(x, axis, [(i, i ^ k) for i in range(size)])


def is_pow2(size):
    return size & (size - 1) == 0


def sum_over(x, axes):
    for axis in axes:
        size = lax.axis_size(axis)
        if not is_pow2(size):
            x = lax.psum(x, axis)
            continue
        k = 1
        while k < size:
            x = x + swap(x, axis, k)
            k *= 2
    return x


def sum_of_four(x, axes):
    size = 1
    for axis in axes:
        size *= lax.axis_size(axis)
    if size != 4:
        return sum_over(x, axes[::-1])
    c, b, a = (lax.ppermute(x, axes, [(i, i ^ k) for i in range(4)]) for k in (3, 2, 1))
    return (c + b) + (a + x)


def totals_kernel(bm, counts, held, total, sem):
    m, n = counts.shape

    def fetch(i):
        rows = pl.ds(i * bm, bm)
        return pltpu.make_async_copy(counts.at[rows, :], held.at[rows, :], sem.at[i])

    for i in range(m // bm):
        fetch(i).start()
    for i in range(m // bm):
        fetch(i).wait()

        def tile(t, acc, i=i):
            return acc + held[pl.ds(i * bm, bm), pl.ds(pl.multiple_of(t * 128, 128), 128)]

        acc = lax.fori_loop(0, n // 128, tile, jnp.zeros((bm, 128), jnp.int32), unroll=8)
        acc = acc.astype(F32)
        for r in range(0, bm, 128):
            row = jnp.sum(acc[r : r + 128].T, axis=0, keepdims=True)
            total[:, i * bm + r : i * bm + r + 128] = row


def column(library, factor, m):
    for t in range(m // 128):
        row = 10000.0 / library[:, t * 128 : (t + 1) * 128]
        factor[t * 128 : (t + 1) * 128, :] = jnp.broadcast_to(row, (128, 128)).T


def stats_kernel(held, library, logged, stats, factor):
    m, n = held.shape
    column(library, factor, m)
    width, bm = 512, 64

    def over_cols(t, carry):
        cols = pl.ds(pl.multiple_of(t * width, width), width)

        def over_rows(r, acc):
            rows = pl.ds(pl.multiple_of(r * bm, bm), bm)
            s = factor[rows, :]
            s = jnp.concatenate([s] * (width // 128), axis=1)
            y = jnp.log2(1.0 + held[rows, cols].astype(F32) * s)
            logged[rows, cols] = y
            parts = y.reshape(bm // 8, 8, width)
            return acc[0] + jnp.sum(parts, axis=0), acc[1] + jnp.sum(parts * parts, axis=0)

        zero = jnp.zeros((8, width), F32)
        one, two = lax.fori_loop(0, m // bm, over_rows, (zero, zero))
        stats[0:1, cols] = jnp.sum(one, axis=0, keepdims=True)
        stats[1:2, cols] = jnp.sum(two, axis=0, keepdims=True)
        return carry

    lax.fori_loop(0, n // width, over_cols, 0)


def two_parts(x):
    h = x.astype(BF16)
    return h, (x - h.astype(F32)).astype(BF16)


def split_kernel(begin, logged, high, low):
    m, n = high.shape
    width, bm = 512, 64

    def over_rows(r, carry):
        rows = pl.ds(pl.multiple_of(r * bm, bm), bm)
        source = pl.ds(pl.multiple_of(begin + r * bm, bm), bm)

        def over_cols(t, c):
            cols = pl.ds(pl.multiple_of(t * width, width), width)
            high[rows, cols], low[rows, cols] = two_parts(logged[source, cols])
            return c

        return lax.fori_loop(0, n // width, over_cols, carry)

    lax.fori_loop(0, m // bm, over_rows, 0)


def mean_scale(stats, ncells):
    mean = stats[0:1, :] / ncells
    meansq = stats[1:2, :] / ncells
    return mean, LN2 / jnp.sqrt((LN2 * LN2) * (meansq - mean * mean) + 1e-05)


def sketch_rows(high, low, weight, shift, at, size):
    rank = weight.shape[1] // 2
    rows = slice(at, at + size)
    acc = jnp.dot(high[rows, :], weight[...], preferred_element_type=F32)
    acc = acc + jnp.dot(low[rows, :], weight[...], preferred_element_type=F32)
    acc = acc.T
    return acc[:rank] + acc[rank:] - shift[:, 0:1]


def away_kernel(ncells, high0, low0, high1, low1, start_t, stats, away, weight, shift):
    q = high0.shape[0] // 2
    mean, scale = mean_scale(stats[...], ncells)
    w = start_t[...] * scale
    shift[...] = jnp.broadcast_to(jnp.sum(w * mean, axis=1, keepdims=True), shift.shape)
    h, l = two_parts(w)
    weight[...] = jnp.concatenate([h, l], axis=0).T
    me = lax.axis_index("sub")

    def half(high, low):
        for i in range(2):
            away[i] = sketch_rows(high, low, weight, shift, i * q, q)

    pl.when(me == 1)(lambda: half(high0, low0))
    pl.when(me == 0)(lambda: half(high1, low1))


def own_kernel(i, high0, low0, high1, low1, weight, shift, own):
    q = high0.shape[0] // 2
    me = lax.axis_index("sub")

    def half(high, low):
        own[...] = sketch_rows(high, low, weight, shift, i * q, q)

    pl.when(me == 0)(lambda: half(high0, low0))
    pl.when(me == 1)(lambda: half(high1, low1))


def prep_kernel(ncells, genes, *refs):
    own0, own1, other0, other1 = refs[:4]
    if genes:
        halves, stats = refs[4:8], refs[8]
    sketch, packed, colsum, gram = refs[-4:]
    rank = own0.shape[0]
    mine = jnp.concatenate([own0[...], own1[...]], axis=1)
    theirs = jnp.concatenate([other0[...], other1[...]], axis=1)
    first = lax.axis_index("sub") == 0
    s = jnp.concatenate([jnp.where(first, mine, theirs), jnp.where(first, theirs, mine)], axis=1)
    sketch[...] = s
    h, l = two_parts(s)
    packed[...] = jnp.concatenate([h, l], axis=0)
    colsum[...] = jnp.broadcast_to(jnp.sum(s, axis=1, keepdims=True), colsum.shape)
    g = lax.dot_general(s, s, NT, precision=HI, preferred_element_type=F32)
    if genes:
        gram[:, :genes] = z_chunk(ncells, 0, genes, packed, colsum, halves, stats)
    gram[:, genes:] = jnp.concatenate([g, g], axis=1)


def eliminate(a, k0, k1):
    row = lax.broadcasted_iota(jnp.int32, (a.shape[0], 1), 0)
    for k in range(k0, k1):
        pivot = a[k : k + 1, :]
        f = a[:, k : k + 1] * (1.0 / a[k : k + 1, k : k + 1])
        a = a - jnp.where(row > k, f, 0.0) * pivot
    return a


def with_identity(gram):
    rank = gram.shape[0]
    lane = lax.broadcasted_iota(jnp.int32, (rank, 2 * rank), 1)
    row = lax.broadcasted_iota(jnp.int32, (rank, 2 * rank), 0)
    return jnp.where(lane < rank, gram, jnp.where(lane - rank == row, 1.0, 0.0))


def lower_inverse(a):
    rank = a.shape[0]
    lane = lax.broadcasted_iota(jnp.int32, (rank, rank), 1)
    row = lax.broadcasted_iota(jnp.int32, (rank, rank), 0)
    diag = jnp.sum(jnp.where(lane == row, a[:, :rank], 0.0), axis=1, keepdims=True)
    return a[:, rank:] * (1.0 / jnp.sqrt(diag))


def inverse_kernel(gram, inverse):
    rank = gram.shape[0]
    inverse[...] = lower_inverse(eliminate(with_identity(gram[...]), 0, rank))


def dot_hi(x, y, dims):
    return lax.dot_general(x, y, dims, precision=HI, preferred_element_type=F32)


def scores_kernel(ncells, sketch, inverse, scores):
    s = lax.dot_general(inverse[...], sketch[...], NN, precision=HI, preferred_element_type=F32)
    scores[...] = s * (float(ncells) ** 0.5)


def z_chunk(ncells, c0, nc, packed, colsum, halves, stats):
    rank = colsum.shape[0]
    half = packed.shape[1] // 2
    cols = slice(c0, c0 + nc)
    z = None
    for i, part in enumerate(halves):
        at = (i // 2) * half
        d = jnp.dot(packed[:, at : at + half], part[:, cols], preferred_element_type=F32)
        z = d if z is None else z + d
    mean, scale = mean_scale(stats[:, cols], ncells)
    return (z[:rank] + z[rank:] - colsum[:, 0:1] * mean) * scale


def product_kernel(ncells, packed, colsum, high0, low0, high1, low1, stats, z):
    n = high0.shape[1]
    nc = min(n, 512)
    halves = (high0, low0, high1, low1)
    for c0 in range(0, n, nc):
        z[:, c0 : c0 + nc] = z_chunk(ncells, c0, nc, packed, colsum, halves, stats)


def dot_parts(x, y, dims):
    xh, xl = two_parts(x)
    yh, yl = two_parts(y)

    def dot(a, b):
        return lax.dot_general(a, b, dims, preferred_element_type=F32)

    return dot(xh, yh) + (dot(xh, yl) + dot(xl, yh))


def finish_kernel(z, inverse, loadings, square):
    l = dot_parts(inverse[...], z[...], NN)
    loadings[...] = l
    square[...] = dot_parts(l, l, NT)


def layout(n):
    tiles = n // 128 + 1
    share = [s * tiles / sum(SHARES) for s in SHARES]
    edges = [round(sum(share[:i])) for i in range(len(share) + 1)]
    sizes = [128 * (b - a) for a, b in zip(edges, edges[1:])]
    return [sizes[0] - 128] + sizes[1:]


def loadings_on_a_line(ncells, sketch, packed, colsum, first, halves, stats):
    rank, n, m = colsum.shape[0], stats.shape[1], sketch.shape[1]
    (lag1, lag2, back), count = LAGS, len(SHARES)
    far = [(i, i ^ 2) for i in range(4)]
    genes = layout(n)
    width = [genes[0] + 2 * rank] + genes[1:]
    begin = [sum(genes[:i]) for i in range(count)]
    pairs = [(0, 1), (1, 0), (2, 3), (3, 2)]
    middle = [(2, 4), (4, 2), (3, 5), (5, 3), (0, 1), (1, 0), (6, 7), (7, 6)]

    slots = count + lag2
    steps = {count + FROM + i: pair for i, pair in enumerate(zip(STEPS, STEPS[1:]))}
    inverted = max(steps)

    def has(i):
        return 0 <= i < count

    def direct(i):
        return count - TAIL <= i < count

    def returns(i):
        return 0 <= i < count - TAIL

    early = {1 + i: count - TAIL + i for i in range(TAIL)}
    finishes, queue = {}, []
    for s in range(slots):
        queue += [d for d in range(count) if d + (lag2 if direct(d) else back) == s]
        take = len(queue) if s > inverted else 0
        finishes[s], queue = queue[:take], queue[take:]

    def chunk(x):
        return jax.ShapeDtypeStruct((rank, x), F32)

    def run(name, ins, outs, kernel):
        def wrapped(*refs):
            kernel(dict(zip(ins, refs)), dict(zip(outs, refs[len(ins) :])))

        results = pl.pallas_call(
            wrapped,
            name=name,
            out_shape=tuple(outs.values()),
            in_specs=[VM] * len(ins),
            out_specs=(VM,) * len(outs),
            compiler_params=params(8),
            cost_estimate=cost(1e9, 1 << 16),
        )(*[val[k] for k in ins])
        val.update(zip(outs, results))

    def at_end():
        z = lax.axis_index("cells")
        return jnp.logical_or(z == 0, z == 3)

    def arrived(d, r):
        if direct(d):
            return r[f"t{d}"][...]
        return jnp.where(at_end(), r[f"down{d}"][:, : width[d]], r[f"t{d}"][...])

    token = jax.ShapeDtypeStruct((8, 128), F32)
    val = dict(token=jnp.zeros((8, 128), F32), square=jnp.zeros((rank, rank), F32))
    val.update(packed=packed, colsum=colsum, stats=stats, z0=first, sketch=sketch)
    val.update(zip(PARTS, halves))

    def main_slot(s, a, b, c):
        ins, outs = ["token"], {"token": token}
        if has(a):
            ins += [f"z{a}"]
        if has(b):
            ins += [f"z{b}", f"up{b}"] + ([f"early{b}"] if direct(b) else [])
            outs[f"s{b}"] = chunk(width[b])
        if has(c):
            ins += [f"s{c}", f"across{c}"]
            outs[f"t{c}"] = chunk(width[c])
        lower = width[c] if returns(c) else width[early[s]] if s in early else 0
        if s in early:
            ins += [f"z{early[s]}"]
        if has(a):
            outs[f"give{s}"] = chunk(max(lower, width[a]))
        if returns(s - back):
            ins += [f"down{s - back}"]

        def kernel(r, o):
            o["token"][...] = r["token"][...]
            if has(b):
                came = r[f"up{b}"][:, : width[b]]
                if direct(b):
                    came = jnp.where(at_end(), r[f"early{b}"][:, : width[b]], came)
                o[f"s{b}"][...] = r[f"z{b}"][...] + came
            if has(c):
                tt = r[f"s{c}"][...] + r[f"across{c}"][...]
                o[f"t{c}"][...] = tt
            if has(a) and lower:
                zz, give = r[f"z{a}"], o[f"give{s}"]
                low = tt if returns(c) else r[f"z{early[s]}"][...]
                least = min(width[a], lower)
                give[:, :least] = jnp.where(at_end(), zz[:, :least], low[:, :least])
                if width[a] > least:
                    give[:, least:] = zz[:, least:]
                if lower > least:
                    give[:, least:] = low[:, least:]
            elif has(a):
                o[f"give{s}"][...] = r[f"z{a}"][...]

        if s:
            run(f"slot{s}", ins, outs, kernel)
        if f"give{s}" in val:
            return val[f"give{s}"]
        return val[f"z{a}"] if has(a) else val[f"t{c}"] if returns(c) else None

    def side_slot(s, a):
        ins, outs = ["token"], {"token": token}
        made = [a] if has(a) and not direct(a) else []
        made += [early[a]] if a in early else []
        if made:
            ins += ["packed", "colsum", "stats", *PARTS]
        for i in made:
            outs[f"z{i}"] = chunk(width[i])
        if s in steps:
            ins += ["t0", "down0"] if steps[s][0] == 0 else ["state"]
            if s == inverted:
                outs["inverse"] = chunk(rank)
            else:
                outs["state"] = chunk(2 * rank)
        if finishes[s]:
            for d in finishes[s]:
                ins += [f"t{d}"] if direct(d) else [f"t{d}", f"down{d}"]
                outs[f"l{d}"] = chunk(genes[d])
            ins += ["square"] if s == inverted else ["inverse", "square"]
            outs["square"] = chunk(rank)
        ins = list(dict.fromkeys(ins))

        def kernel(r, o):
            o["token"][...] = r["token"][...]
            for i in made:
                o[f"z{i}"][...] = z_chunk(
                    ncells,
                    begin[i],
                    genes[i],
                    r["packed"],
                    r["colsum"],
                    [r[k] for k in PARTS],
                    r["stats"],
                )
            if s in steps:
                if steps[s][0] == 0:
                    x = with_identity(arrived(0, r)[:, -2 * rank :])
                else:
                    x = r["state"][...]
                x = eliminate(x, *steps[s])
                if s == inverted:
                    x = lower_inverse(x)
                    o["inverse"][...] = x
                else:
                    o["state"][...] = x
            if finishes[s]:
                total = r["square"][...]
                inverse = x if s == inverted else r["inverse"][...]
                for d in finishes[s]:
                    l = dot_parts(inverse, arrived(d, r)[:, : genes[d]], NN)
                    o[f"l{d}"][...] = l
                    total = total + dot_parts(l, l, NT)
                o["square"][...] = total

        if len(outs) > 1:
            run(f"side{s}", ins, outs, kernel)

    for s in range(slots):
        a, b, c = s, s - lag1, s - lag2
        give = main_slot(s, a, b, c)
        if give is not None:
            got = lax.ppermute(give, "cells", pairs)
            if has(a):
                val[f"up{a}"] = got
            if s in early:
                val[f"early{early[s]}"] = got
            if returns(c):
                val[f"down{c}"] = got
        if has(b) and direct(b):
            val[f"across{b}"] = lax.ppermute(val[f"s{b}"], "cells", far)
        elif has(b):
            val[f"across{b}"] = lax.ppermute(val[f"s{b}"], ("cells", "sub"), middle)
        side_slot(s, a + 1)

    def last(r, o):
        o["scores"][...] = dot_parts(r["inverse"][...], r["sketch"][...], NN) * (
            float(ncells) ** 0.5
        )
        for d in range(count):
            o["loadings"][:, begin[d] : begin[d] + genes[d]] = r[f"l{d}"][...]

    pieces = [f"l{d}" for d in range(count)]
    run("last", ["token", "inverse", "sketch"] + pieces, dict(scores=chunk(m), loadings=chunk(n)), last)
    return val["loadings"], val["square"], val["scores"]


PARTS = ("high0", "low0", "high1", "low1")
LAGS = (2, 4, 6)
TAIL = 2
SHARES = (4, 4, 5, 5, 5, 4, 3, 3)
STEPS = (0, 16, 32, 64)
FROM = -1


def call(kernel, name, out_shape, args, scratch=(), mib=4, flops=0, nbytes=MIB):
    single = not isinstance(out_shape, tuple)
    return pl.pallas_call(
        kernel,
        name=name,
        out_shape=out_shape,
        in_specs=[VM] * len(args),
        out_specs=VM if single else (VM,) * len(out_shape),
        scratch_shapes=list(scratch),
        compiler_params=params(mib),
        cost_estimate=cost(flops, nbytes),
    )(*args)


def f32(*shape):
    return jax.ShapeDtypeStruct(shape, F32)


def body(counts, start_block):
    m, n = counts.shape
    rank = start_block.shape[1]
    cells = lax.axis_size("cells")
    ncells = m * cells
    genes = n * lax.axis_size("genes") * lax.axis_size("sub")

    bm = 128
    held, total = pl.pallas_call(
        functools.partial(totals_kernel, bm),
        name="totals",
        out_shape=(pltpu.VMEM((m, n), jnp.int32), f32(1, m)),
        in_specs=[pl.BlockSpec(memory_space=pltpu.HBM)],
        out_specs=(VM, VM),
        scratch_shapes=[pltpu.SemaphoreType.DMA((m // bm,))],
        compiler_params=params(4),
        cost_estimate=cost(0, 24 * m * n),
    )(pltpu.with_memory_space_constraint(counts, pltpu.HBM))
    library = sum_of_four(total, ("genes", "sub"))

    logged, stats = call(
        stats_kernel,
        "stats",
        (pltpu.VMEM((m, n), F32), f32(2, n)),
        [vmem(held), library],
        [pltpu.VMEM((m, 128), F32)],
        nbytes=20 * m * n,
    )
    logged = vmem(logged)

    halves = []
    for i in range(2):
        halves += call(
            functools.partial(split_kernel, i * (m // 2)),
            "split",
            (pltpu.VMEM((m // 2, n), BF16), pltpu.VMEM((m // 2, n), BF16)),
            [logged],
            nbytes=4 * m * n,
        )
    stats = sum_of_four(stats, ("cells",))

    halves = [vmem(x) for x in halves]
    away, weight, shift = call(
        functools.partial(away_kernel, ncells),
        "away",
        (f32(2, rank, m // 4), jax.ShapeDtypeStruct((n, 2 * rank), BF16), f32(rank, 128)),
        [*halves, start_block.T, stats],
        flops=4 * m * n * rank,
        mib=8,
    )
    away = swap(away, "sub")
    own, other = [], []
    for i in range(2):
        part = call(
            functools.partial(own_kernel, i),
            "own",
            f32(rank, m // 4),
            [*halves, weight, shift],
            flops=2 * m * n * rank,
        )
        own.append(sum_over(part + away[i], ("genes",)))
        other.append(swap(own[i], "sub"))

    line = cells == 4 and n % 1024 == 0 and 2 * rank == 128
    genes0 = layout(n)[0] if line else 0
    sketch, packed, colsum, gram = call(
        functools.partial(prep_kernel, ncells, genes0),
        "prep",
        (
            f32(rank, m),
            jax.ShapeDtypeStruct((2 * rank, m), BF16),
            f32(rank, 128),
            f32(rank, genes0 + 2 * rank),
        ),
        own + other + ([*halves, stats] if line else []),
        flops=12 * m * rank * rank,
        mib=8,
    )

    if line:
        loadings, square, scores = loadings_on_a_line(
            ncells, sketch, packed, colsum, gram, halves, stats
        )
    else:
        z = call(
            functools.partial(product_kernel, ncells),
            "product",
            f32(rank, n),
            [packed, colsum, *halves, stats],
            mib=8,
        )
        inverse = call(
            inverse_kernel, "inverse", f32(rank, rank), [sum_over(gram, ("cells",))]
        )
        loadings, square = call(
            finish_kernel,
            "finish",
            (f32(rank, n), f32(rank, rank)),
            [lax.psum(z, "cells"), inverse],
            mib=16,
        )
        scores = call(
            functools.partial(scores_kernel, ncells), "scores", f32(rank, m), [sketch, inverse]
        )
    ritz = sum_of_four(square, ("genes", "sub")) / genes
    return (scores.T, loadings.T, ritz)


def solution(mesh):
    placed = (P(("groups", "cells"), ("genes", "sub")), P(("genes", "sub"), None))
    return jax.shard_map(
        body,
        mesh=mesh,
        in_specs=placed,
        out_specs=(
            P(("groups", "cells"), None),
            P(("groups", "genes", "sub"), None),
            P("groups", None),
        ),
        check_vma=False,
    )
```

```python
import functools

import jax
import jax.numpy as jnp
from jax import lax
from jax.experimental import pallas as pl
from jax.experimental.pallas import tpu as pltpu
from jax.sharding import PartitionSpec as P

F32 = jnp.float32
BF16 = jnp.bfloat16
HI = lax.Precision.HIGHEST
VM = pl.BlockSpec(memory_space=pltpu.VMEM)
SM = pl.BlockSpec(memory_space=pltpu.SMEM)
ANY = pl.BlockSpec(memory_space=pl.ANY)
MIB = 1 << 20
LN2 = 0.6931471805599453
NT = (((1,), (1,)), ((), ()))
NN = (((1,), (0,)), ((), ()))


def params(mib=16):
    return pltpu.CompilerParams(vmem_limit_bytes=mib * MIB)


def vmem(x):
    return pltpu.with_memory_space_constraint(x, pltpu.VMEM)


def cost(flops, nbytes):
    return pl.CostEstimate(flops=int(flops), bytes_accessed=int(nbytes), transcendentals=0)


def swap(x, axis, k=1):
    size = lax.axis_size(axis)
    return lax.ppermute(x, axis, [(i, i ^ k) for i in range(size)])


def is_pow2(size):
    return size & (size - 1) == 0


def sum_over(x, axes):
    for axis in axes:
        size = lax.axis_size(axis)
        if not is_pow2(size):
            x = lax.psum(x, axis)
            continue
        k = 1
        while k < size:
            x = x + swap(x, axis, k)
            k *= 2
    return x


def sum_of_four(x, axes):
    size = 1
    for axis in axes:
        size *= lax.axis_size(axis)
    if size != 4:
        return sum_over(x, axes[::-1])
    c, b, a = (lax.ppermute(x, axes, [(i, i ^ k) for i in range(4)]) for k in (3, 2, 1))
    return (c + b) + (a + x)


def totals_kernel(bm, counts, held, total, sem):
    m, n = counts.shape

    def fetch(i):
        rows = pl.ds(i * bm, bm)
        return pltpu.make_async_copy(counts.at[rows, :], held.at[rows, :], sem.at[i])

    for i in range(m // bm):
        fetch(i).start()
    for i in range(m // bm):
        fetch(i).wait()

        def tile(t, acc, i=i):
            return acc + held[pl.ds(i * bm, bm), pl.ds(pl.multiple_of(t * 128, 128), 128)]

        acc = lax.fori_loop(0, n // 128, tile, jnp.zeros((bm, 128), jnp.int32), unroll=8)
        acc = acc.astype(F32)
        for r in range(0, bm, 128):
            row = jnp.sum(acc[r : r + 128].T, axis=0, keepdims=True)
            total[:, i * bm + r : i * bm + r + 128] = row


def column(library, factor, m):
    for t in range(m // 128):
        row = 10000.0 / library[:, t * 128 : (t + 1) * 128]
        factor[t * 128 : (t + 1) * 128, :] = jnp.broadcast_to(row, (128, 128)).T


def stats_kernel(held, library, logged, stats, factor):
    m, n = held.shape
    column(library, factor, m)
    width, bm = 512, 64

    def over_cols(t, carry):
        cols = pl.ds(pl.multiple_of(t * width, width), width)

        def over_rows(r, acc):
            rows = pl.ds(pl.multiple_of(r * bm, bm), bm)
            s = factor[rows, :]
            s = jnp.concatenate([s] * (width // 128), axis=1)
            y = jnp.log2(1.0 + held[rows, cols].astype(F32) * s)
            logged[rows, cols] = y
            parts = y.reshape(bm // 8, 8, width)
            return acc[0] + jnp.sum(parts, axis=0), acc[1] + jnp.sum(parts * parts, axis=0)

        zero = jnp.zeros((8, width), F32)
        one, two = lax.fori_loop(0, m // bm, over_rows, (zero, zero))
        stats[0:1, cols] = jnp.sum(one, axis=0, keepdims=True)
        stats[1:2, cols] = jnp.sum(two, axis=0, keepdims=True)
        return carry

    lax.fori_loop(0, n // width, over_cols, 0)


def two_parts(x):
    h = x.astype(BF16)
    return h, (x - h.astype(F32)).astype(BF16)


def split_kernel(begin, logged, high, low):
    m, n = high.shape
    width, bm = 512, 64

    def over_rows(r, carry):
        rows = pl.ds(pl.multiple_of(r * bm, bm), bm)
        source = pl.ds(pl.multiple_of(begin + r * bm, bm), bm)

        def over_cols(t, c):
            cols = pl.ds(pl.multiple_of(t * width, width), width)
            high[rows, cols], low[rows, cols] = two_parts(logged[source, cols])
            return c

        return lax.fori_loop(0, n // width, over_cols, carry)

    lax.fori_loop(0, m // bm, over_rows, 0)


def mean_scale(stats, ncells):
    mean = stats[0:1, :] / ncells
    meansq = stats[1:2, :] / ncells
    return mean, LN2 / jnp.sqrt((LN2 * LN2) * (meansq - mean * mean) + 1e-05)


def sketch_half(high, low, weight, shift, out):
    rank = weight.shape[1] // 2
    half = high.shape[0]
    both = jnp.concatenate([high[...], low[...]], axis=0)
    acc = jnp.dot(both, weight[...], preferred_element_type=F32)
    acc = (acc[:half] + acc[half:]).T
    acc = acc[:rank] + acc[rank:] - shift[:, 0:1]
    for i in range(2):
        out[i] = acc[:, i * (half // 2) : (i + 1) * (half // 2)]


def away_kernel(ncells, high0, low0, high1, low1, start_t, stats, away, weight, shift):
    mean, scale = mean_scale(stats[...], ncells)
    w = start_t[...] * scale
    shift[...] = jnp.broadcast_to(jnp.sum(w * mean, axis=1, keepdims=True), shift.shape)
    h, l = two_parts(w)
    weight[...] = jnp.concatenate([h, l], axis=0).T
    me = lax.axis_index("sub")
    pl.when(me == 1)(lambda: sketch_half(high0, low0, weight, shift, away))
    pl.when(me == 0)(lambda: sketch_half(high1, low1, weight, shift, away))


def own_kernel(high0, low0, high1, low1, weight, shift, own):
    me = lax.axis_index("sub")
    pl.when(me == 0)(lambda: sketch_half(high0, low0, weight, shift, own))
    pl.when(me == 1)(lambda: sketch_half(high1, low1, weight, shift, own))


def prep_kernel(ncells, genes, *refs):
    own0, own1, other0, other1 = refs[:4]
    if genes:
        halves, stats = refs[4:8], refs[8]
    sketch, packed, colsum, gram = refs[-4:]
    rank = own0.shape[0]
    mine = jnp.concatenate([own0[...], own1[...]], axis=1)
    theirs = jnp.concatenate([other0[...], other1[...]], axis=1)
    first = lax.axis_index("sub") == 0
    s = jnp.concatenate([jnp.where(first, mine, theirs), jnp.where(first, theirs, mine)], axis=1)
    sketch[...] = s
    h, l = two_parts(s)
    packed[...] = jnp.concatenate([h, l], axis=0)
    colsum[...] = jnp.broadcast_to(jnp.sum(s, axis=1, keepdims=True), colsum.shape)
    g = lax.dot_general(s, s, NT, precision=HI, preferred_element_type=F32)
    if genes:
        gram[:, :genes] = z_chunk(ncells, 0, genes, packed, colsum, halves, stats)
    gram[:, genes:] = jnp.concatenate([g, g], axis=1)


def eliminate(a, k0, k1):
    rank = a.shape[0]
    a = a.reshape(rank // 8, 8, 2 * rank)
    row = 8 * lax.broadcasted_iota(jnp.int32, a.shape, 0)
    row = row + lax.broadcasted_iota(jnp.int32, a.shape, 1)

    def wide(x):
        return jnp.broadcast_to(x, a.shape[1:])

    for k in range(k0, k1, 8):
        block = a[k // 8]
        p = [wide(block[j : j + 1, :]) for j in range(8)]
        s = [[wide(block[i : i + 1, k + j : k + j + 1]) for j in range(8)] for i in range(8)]
        c = [jnp.broadcast_to(a[:, :, k + j : k + j + 1], a.shape) for j in range(8)]
        for j in range(8):
            r = 1.0 / s[j][j]
            f = c[j] * r[None]
            for t in range(j + 1, 8):
                l = s[t][j] * r
                p[t] = p[t] - l * p[j]
                for u in range(j + 1, 8):
                    s[t][u] = s[t][u] - l * s[j][u]
                c[t] = c[t] - f * s[j][t][None]
            a = a - jnp.where(row > k + j, f, 0.0) * p[j][None]
    return a.reshape(rank, 2 * rank)


def with_identity(gram):
    rank = gram.shape[0]
    lane = lax.broadcasted_iota(jnp.int32, (rank, 2 * rank), 1)
    row = lax.broadcasted_iota(jnp.int32, (rank, 2 * rank), 0)
    return jnp.where(lane < rank, gram, jnp.where(lane - rank == row, 1.0, 0.0))


def lower_inverse(a):
    rank = a.shape[0]
    lane = lax.broadcasted_iota(jnp.int32, (rank, rank), 1)
    row = lax.broadcasted_iota(jnp.int32, (rank, rank), 0)
    diag = jnp.sum(jnp.where(lane == row, a[:, :rank], 0.0), axis=1, keepdims=True)
    return a[:, rank:] * (1.0 / jnp.sqrt(diag))


def inverse_kernel(gram, inverse):
    rank = gram.shape[0]
    inverse[...] = lower_inverse(eliminate(with_identity(gram[...]), 0, rank))


def dot_hi(x, y, dims):
    return lax.dot_general(x, y, dims, precision=HI, preferred_element_type=F32)


def scores_kernel(ncells, sketch, inverse, scores):
    s = lax.dot_general(inverse[...], sketch[...], NN, precision=HI, preferred_element_type=F32)
    scores[...] = s * (float(ncells) ** 0.5)


def z_chunk(ncells, c0, nc, packed, colsum, halves, stats):
    rank = colsum.shape[0]
    half = packed.shape[1] // 2
    cols = slice(c0, c0 + nc)
    z = None
    for i, part in enumerate(halves):
        at = (i // 2) * half
        d = jnp.dot(packed[:, at : at + half], part[:, cols], preferred_element_type=F32)
        z = d if z is None else z + d
    mean, scale = mean_scale(stats[:, cols], ncells)
    return (z[:rank] + z[rank:] - colsum[:, 0:1] * mean) * scale


def product_kernel(ncells, packed, colsum, high0, low0, high1, low1, stats, z):
    n = high0.shape[1]
    nc = min(n, 512)
    halves = (high0, low0, high1, low1)
    for c0 in range(0, n, nc):
        z[:, c0 : c0 + nc] = z_chunk(ncells, c0, nc, packed, colsum, halves, stats)


def dot_parts(x, y, dims):
    xh, xl = two_parts(x)
    yh, yl = two_parts(y)

    def dot(a, b):
        return lax.dot_general(a, b, dims, preferred_element_type=F32)

    return dot(xh, yh) + (dot(xh, yl) + dot(xl, yh))


def finish_kernel(z, inverse, loadings, square):
    l = dot_parts(inverse[...], z[...], NN)
    loadings[...] = l
    square[...] = dot_parts(l, l, NT)


def layout(n):
    tiles = n // 128 + 1
    share = [s * tiles / sum(SHARES) for s in SHARES]
    edges = [round(sum(share[:i])) for i in range(len(share) + 1)]
    sizes = [128 * (b - a) for a, b in zip(edges, edges[1:])]
    return [sizes[0] - 128] + sizes[1:]


def loadings_on_a_line(ncells, sketch, packed, colsum, first, halves, stats):
    rank, n, m = colsum.shape[0], stats.shape[1], sketch.shape[1]
    (lag1, lag2, back), count = LAGS, len(SHARES)
    far = [(i, i ^ 2) for i in range(4)]
    genes = layout(n)
    width = [genes[0] + 2 * rank] + genes[1:]
    begin = [sum(genes[:i]) for i in range(count)]
    pairs = [(0, 1), (1, 0), (2, 3), (3, 2)]
    middle = [(2, 4), (4, 2), (3, 5), (5, 3), (0, 1), (1, 0), (6, 7), (7, 6)]

    slots = count + lag2
    steps = {count + FROM + i: pair for i, pair in enumerate(zip(STEPS, STEPS[1:]))}
    inverted = max(steps)

    def has(i):
        return 0 <= i < count

    def direct(i):
        return count - TAIL <= i < count

    def returns(i):
        return 0 <= i < count - TAIL

    early = {1 + i: count - TAIL + i for i in range(TAIL)}
    finishes, queue = {}, []
    for s in range(slots):
        queue += [d for d in range(count) if d + (lag2 if direct(d) else back) == s]
        take = len(queue) if s > inverted else 0
        finishes[s], queue = queue[:take], queue[take:]

    def chunk(x):
        return jax.ShapeDtypeStruct((rank, x), F32)

    def run(name, ins, outs, kernel):
        def wrapped(*refs):
            kernel(dict(zip(ins, refs)), dict(zip(outs, refs[len(ins) :])))

        results = pl.pallas_call(
            wrapped,
            name=name,
            out_shape=tuple(outs.values()),
            in_specs=[VM] * len(ins),
            out_specs=(VM,) * len(outs),
            compiler_params=params(8),
            cost_estimate=cost(1e9, 1 << 16),
        )(*[val[k] for k in ins])
        val.update(zip(outs, results))

    def at_end():
        z = lax.axis_index("cells")
        return jnp.logical_or(z == 0, z == 3)

    def arrived(d, r):
        if direct(d):
            return r[f"t{d}"][...]
        return jnp.where(at_end(), r[f"down{d}"][:, : width[d]], r[f"t{d}"][...])

    token = jax.ShapeDtypeStruct((8, 128), F32)
    val = dict(token=jnp.zeros((8, 128), F32), square=jnp.zeros((rank, rank), F32))
    val.update(packed=packed, colsum=colsum, stats=stats, z0=first, sketch=sketch)
    val.update(zip(PARTS, halves))

    def main_slot(s, a, b, c):
        ins, outs = ["token"], {"token": token}
        if has(a):
            ins += [f"z{a}"]
        if has(b):
            ins += [f"z{b}", f"up{b}"] + ([f"early{b}"] if direct(b) else [])
            outs[f"s{b}"] = chunk(width[b])
        if has(c):
            ins += [f"s{c}", f"across{c}"]
            outs[f"t{c}"] = chunk(width[c])
        lower = width[c] if returns(c) else width[early[s]] if s in early else 0
        if s in early:
            ins += [f"z{early[s]}"]
        if has(a):
            outs[f"give{s}"] = chunk(max(lower, width[a]))
        if returns(s - back):
            ins += [f"down{s - back}"]

        def kernel(r, o):
            o["token"][...] = r["token"][...]
            if has(b):
                came = r[f"up{b}"][:, : width[b]]
                if direct(b):
                    came = jnp.where(at_end(), r[f"early{b}"][:, : width[b]], came)
                o[f"s{b}"][...] = r[f"z{b}"][...] + came
            if has(c):
                tt = r[f"s{c}"][...] + r[f"across{c}"][...]
                o[f"t{c}"][...] = tt
            if has(a) and lower:
                zz, give = r[f"z{a}"], o[f"give{s}"]
                low = tt if returns(c) else r[f"z{early[s]}"][...]
                least = min(width[a], lower)
                give[:, :least] = jnp.where(at_end(), zz[:, :least], low[:, :least])
                if width[a] > least:
                    give[:, least:] = zz[:, least:]
                if lower > least:
                    give[:, least:] = low[:, least:]
            elif has(a):
                o[f"give{s}"][...] = r[f"z{a}"][...]

        if s:
            run(f"slot{s}", ins, outs, kernel)
        if f"give{s}" in val:
            return val[f"give{s}"]
        return val[f"z{a}"] if has(a) else val[f"t{c}"] if returns(c) else None

    def side_slot(s, a):
        ins, outs = ["token"], {"token": token}
        made = [a] if has(a) and not direct(a) else []
        made += [early[a]] if a in early else []
        if made:
            ins += ["packed", "colsum", "stats", *PARTS]
        for i in made:
            outs[f"z{i}"] = chunk(width[i])
        if s in steps:
            ins += ["t0", "down0"] if steps[s][0] == 0 else ["state"]
            if s == inverted:
                outs["inverse"] = chunk(rank)
            else:
                outs["state"] = chunk(2 * rank)
        if finishes[s]:
            for d in finishes[s]:
                ins += [f"t{d}"] if direct(d) else [f"t{d}", f"down{d}"]
                outs[f"l{d}"] = chunk(genes[d])
            ins += ["square"] if s == inverted else ["inverse", "square"]
            outs["square"] = chunk(rank)
        ins = list(dict.fromkeys(ins))

        def kernel(r, o):
            o["token"][...] = r["token"][...]
            for i in made:
                o[f"z{i}"][...] = z_chunk(
                    ncells,
                    begin[i],
                    genes[i],
                    r["packed"],
                    r["colsum"],
                    [r[k] for k in PARTS],
                    r["stats"],
                )
            if s in steps:
                if steps[s][0] == 0:
                    x = with_identity(arrived(0, r)[:, -2 * rank :])
                else:
                    x = r["state"][...]
                x = eliminate(x, *steps[s])
                if s == inverted:
                    x = lower_inverse(x)
                    o["inverse"][...] = x
                else:
                    o["state"][...] = x
            if finishes[s]:
                total = r["square"][...]
                inverse = x if s == inverted else r["inverse"][...]
                for d in finishes[s]:
                    l = dot_parts(inverse, arrived(d, r)[:, : genes[d]], NN)
                    o[f"l{d}"][...] = l
                    total = total + dot_parts(l, l, NT)
                o["square"][...] = total

        if len(outs) > 1:
            run(f"side{s}", ins, outs, kernel)

    for s in range(slots):
        a, b, c = s, s - lag1, s - lag2
        give = main_slot(s, a, b, c)
        if give is not None:
            got = lax.ppermute(give, "cells", pairs)
            if has(a):
                val[f"up{a}"] = got
            if s in early:
                val[f"early{early[s]}"] = got
            if returns(c):
                val[f"down{c}"] = got
        if has(b) and direct(b):
            val[f"across{b}"] = lax.ppermute(val[f"s{b}"], "cells", far)
        elif has(b):
            val[f"across{b}"] = lax.ppermute(val[f"s{b}"], ("cells", "sub"), middle)
        side_slot(s, a + 1)

    def last(r, o):
        o["scores"][...] = dot_parts(r["inverse"][...], r["sketch"][...], NN) * (
            float(ncells) ** 0.5
        )
        for d in range(count):
            o["loadings"][:, begin[d] : begin[d] + genes[d]] = r[f"l{d}"][...]

    pieces = [f"l{d}" for d in range(count)]
    run("last", ["token", "inverse", "sketch"] + pieces, dict(scores=chunk(m), loadings=chunk(n)), last)
    return val["loadings"], val["square"], val["scores"]


PARTS = ("high0", "low0", "high1", "low1")
LAGS = (2, 4, 6)
TAIL = 2
SHARES = (3, 4, 4, 4, 4, 4, 4, 3, 3)
STEPS = (0, 64)
FROM = 1


def call(kernel, name, out_shape, args, scratch=(), mib=4, flops=0, nbytes=MIB):
    single = not isinstance(out_shape, tuple)
    return pl.pallas_call(
        kernel,
        name=name,
        out_shape=out_shape,
        in_specs=[VM] * len(args),
        out_specs=VM if single else (VM,) * len(out_shape),
        scratch_shapes=list(scratch),
        compiler_params=params(mib),
        cost_estimate=cost(flops, nbytes),
    )(*args)


def f32(*shape):
    return jax.ShapeDtypeStruct(shape, F32)


def body(counts, start_block):
    m, n = counts.shape
    rank = start_block.shape[1]
    cells = lax.axis_size("cells")
    ncells = m * cells
    genes = n * lax.axis_size("genes") * lax.axis_size("sub")

    bm = 128
    held, total = pl.pallas_call(
        functools.partial(totals_kernel, bm),
        name="totals",
        out_shape=(pltpu.VMEM((m, n), jnp.int32), f32(1, m)),
        in_specs=[pl.BlockSpec(memory_space=pltpu.HBM)],
        out_specs=(VM, VM),
        scratch_shapes=[pltpu.SemaphoreType.DMA((m // bm,))],
        compiler_params=params(4),
        cost_estimate=cost(0, 24 * m * n),
    )(pltpu.with_memory_space_constraint(counts, pltpu.HBM))
    library = sum_of_four(total, ("genes", "sub"))

    logged, stats = call(
        stats_kernel,
        "stats",
        (pltpu.VMEM((m, n), F32), f32(2, n)),
        [vmem(held), library],
        [pltpu.VMEM((m, 128), F32)],
        nbytes=20 * m * n,
    )
    logged = vmem(logged)

    halves = []
    for i in range(2):
        halves += call(
            functools.partial(split_kernel, i * (m // 2)),
            "split",
            (pltpu.VMEM((m // 2, n), BF16), pltpu.VMEM((m // 2, n), BF16)),
            [logged],
            nbytes=4 * m * n,
        )
    stats = sum_of_four(stats, ("cells",))

    halves = [vmem(x) for x in halves]
    away, weight, shift = call(
        functools.partial(away_kernel, ncells),
        "away",
        (f32(2, rank, m // 4), jax.ShapeDtypeStruct((n, 2 * rank), BF16), f32(rank, 128)),
        [*halves, start_block.T, stats],
        flops=4 * m * n * rank,
        mib=8,
    )
    away = swap(away, "sub")
    part = call(
        own_kernel,
        "own",
        f32(2, rank, m // 4),
        [*halves, weight, shift],
        flops=4 * m * n * rank,
        mib=8,
    )
    own, other = [], []
    for i in range(2):
        own.append(sum_over(part[i] + away[i], ("genes",)))
        other.append(swap(own[i], "sub"))

    line = cells == 4 and n % 1024 == 0 and 2 * rank == 128
    genes0 = layout(n)[0] if line else 0
    sketch, packed, colsum, gram = call(
        functools.partial(prep_kernel, ncells, genes0),
        "prep",
        (
            f32(rank, m),
            jax.ShapeDtypeStruct((2 * rank, m), BF16),
            f32(rank, 128),
            f32(rank, genes0 + 2 * rank),
        ),
        own + other + ([*halves, stats] if line else []),
        flops=12 * m * rank * rank,
        mib=8,
    )

    if line:
        loadings, square, scores = loadings_on_a_line(
            ncells, sketch, packed, colsum, gram, halves, stats
        )
    else:
        z = call(
            functools.partial(product_kernel, ncells),
            "product",
            f32(rank, n),
            [packed, colsum, *halves, stats],
            mib=8,
        )
        inverse = call(
            inverse_kernel, "inverse", f32(rank, rank), [sum_over(gram, ("cells",))]
        )
        loadings, square = call(
            finish_kernel,
            "finish",
            (f32(rank, n), f32(rank, rank)),
            [lax.psum(z, "cells"), inverse],
            mib=16,
        )
        scores = call(
            functools.partial(scores_kernel, ncells), "scores", f32(rank, m), [sketch, inverse]
        )
    ritz = sum_of_four(square, ("genes", "sub")) / genes
    return (scores.T, loadings.T, ritz)


def solution(mesh):
    placed = (P(("groups", "cells"), ("genes", "sub")), P(("genes", "sub"), None))
    return jax.shard_map(
        body,
        mesh=mesh,
        in_specs=placed,
        out_specs=(
            P(("groups", "cells"), None),
            P(("groups", "genes", "sub"), None),
            P("groups", None),
        ),
        check_vma=False,
    )
```

```python
import functools

import jax
import jax.numpy as jnp
from jax import lax
from jax.experimental import pallas as pl
from jax.experimental.pallas import tpu as pltpu
from jax.sharding import PartitionSpec as P

F32 = jnp.float32
BF16 = jnp.bfloat16
HI = lax.Precision.HIGHEST
VM = pl.BlockSpec(memory_space=pltpu.VMEM)
SM = pl.BlockSpec(memory_space=pltpu.SMEM)
ANY = pl.BlockSpec(memory_space=pl.ANY)
MIB = 1 << 20
LN2 = 0.6931471805599453
NT = (((1,), (1,)), ((), ()))
NN = (((1,), (0,)), ((), ()))


def params(mib=16):
    return pltpu.CompilerParams(vmem_limit_bytes=mib * MIB)


def vmem(x):
    return pltpu.with_memory_space_constraint(x, pltpu.VMEM)


def cost(flops, nbytes):
    return pl.CostEstimate(flops=int(flops), bytes_accessed=int(nbytes), transcendentals=0)


def swap(x, axis, k=1):
    size = lax.axis_size(axis)
    return lax.ppermute(x, axis, [(i, i ^ k) for i in range(size)])


def is_pow2(size):
    return size & (size - 1) == 0


def sum_over(x, axes):
    for axis in axes:
        size = lax.axis_size(axis)
        if not is_pow2(size):
            x = lax.psum(x, axis)
            continue
        k = 1
        while k < size:
            x = x + swap(x, axis, k)
            k *= 2
    return x


def sum_of_four(x, axes):
    size = 1
    for axis in axes:
        size *= lax.axis_size(axis)
    if size != 4:
        return sum_over(x, axes[::-1])
    c, b, a = (lax.ppermute(x, axes, [(i, i ^ k) for i in range(4)]) for k in (3, 2, 1))
    return (c + b) + (a + x)


def totals_kernel(bm, counts, held, total, sem):
    m, n = counts.shape

    def fetch(i):
        rows = pl.ds(i * bm, bm)
        return pltpu.make_async_copy(counts.at[rows, :], held.at[rows, :], sem.at[i])

    for i in range(m // bm):
        fetch(i).start()
    for i in range(m // bm):
        fetch(i).wait()

        def tile(t, acc, i=i):
            return acc + held[pl.ds(i * bm, bm), pl.ds(pl.multiple_of(t * 128, 128), 128)]

        acc = lax.fori_loop(0, n // 128, tile, jnp.zeros((bm, 128), jnp.int32), unroll=8)
        acc = acc.astype(F32)
        for r in range(0, bm, 128):
            row = jnp.sum(acc[r : r + 128].T, axis=0, keepdims=True)
            total[:, i * bm + r : i * bm + r + 128] = row


def column(library, factor, m):
    for t in range(m // 128):
        row = 10000.0 / library[:, t * 128 : (t + 1) * 128]
        factor[t * 128 : (t + 1) * 128, :] = jnp.broadcast_to(row, (128, 128)).T


def stats_kernel(held, library, logged, stats, factor):
    m, n = held.shape
    column(library, factor, m)
    width = 512

    def over_cols(t, carry):
        cols = pl.ds(pl.multiple_of(t * width, width), width)
        s = jnp.concatenate([factor[...]] * (width // 128), axis=1)
        y = jnp.log2(1.0 + held[:, cols].astype(F32) * s)
        logged[:, cols] = y
        parts = y.reshape(m // 8, 8, width)
        one, two = jnp.sum(parts, axis=0), jnp.sum(parts * parts, axis=0)
        stats[0:1, cols] = jnp.sum(one, axis=0, keepdims=True)
        stats[1:2, cols] = jnp.sum(two, axis=0, keepdims=True)
        return carry

    lax.fori_loop(0, n // width, over_cols, 0)


def two_parts(x):
    h = x.astype(BF16)
    return h, (x - h.astype(F32)).astype(BF16)


def split_kernel(begin, logged, high, low):
    m, n = high.shape
    width, bm = 512, 64

    def over_rows(r, carry):
        rows = pl.ds(pl.multiple_of(r * bm, bm), bm)
        source = pl.ds(pl.multiple_of(begin + r * bm, bm), bm)

        def over_cols(t, c):
            cols = pl.ds(pl.multiple_of(t * width, width), width)
            high[rows, cols], low[rows, cols] = two_parts(logged[source, cols])
            return c

        return lax.fori_loop(0, n // width, over_cols, carry)

    lax.fori_loop(0, m // bm, over_rows, 0)


def mean_scale(stats, ncells):
    mean = stats[0:1, :] / ncells
    meansq = stats[1:2, :] / ncells
    return mean, LN2 / jnp.sqrt((LN2 * LN2) * (meansq - mean * mean) + 1e-05)


def sketch_half(high, low, weight, shift, out):
    rank = weight.shape[1] // 2
    half = high.shape[0]
    both = jnp.concatenate([high[...], low[...]], axis=0)
    acc = jnp.dot(both, weight[...], preferred_element_type=F32)
    acc = (acc[:half] + acc[half:]).T
    acc = acc[:rank] + acc[rank:] - shift[:, 0:1]
    for i in range(2):
        out[i] = acc[:, i * (half // 2) : (i + 1) * (half // 2)]


def away_kernel(ncells, high0, low0, high1, low1, start_t, stats, away, weight, shift):
    mean, scale = mean_scale(stats[...], ncells)
    w = start_t[...] * scale
    shift[...] = jnp.broadcast_to(jnp.sum(w * mean, axis=1, keepdims=True), shift.shape)
    h, l = two_parts(w)
    weight[...] = jnp.concatenate([h, l], axis=0).T
    me = lax.axis_index("sub")
    pl.when(me == 1)(lambda: sketch_half(high0, low0, weight, shift, away))
    pl.when(me == 0)(lambda: sketch_half(high1, low1, weight, shift, away))


def own_kernel(high0, low0, high1, low1, weight, shift, own):
    me = lax.axis_index("sub")
    pl.when(me == 0)(lambda: sketch_half(high0, low0, weight, shift, own))
    pl.when(me == 1)(lambda: sketch_half(high1, low1, weight, shift, own))


def prep_kernel(ncells, genes, *refs):
    own0, own1, other0, other1 = refs[:4]
    if genes:
        halves, stats = refs[4:8], refs[8]
    sketch, packed, colsum, gram = refs[-4:]
    rank = own0.shape[0]
    mine = jnp.concatenate([own0[...], own1[...]], axis=1)
    theirs = jnp.concatenate([other0[...], other1[...]], axis=1)
    first = lax.axis_index("sub") == 0
    s = jnp.concatenate([jnp.where(first, mine, theirs), jnp.where(first, theirs, mine)], axis=1)
    sketch[...] = s
    h, l = two_parts(s)
    packed[...] = jnp.concatenate([h, l], axis=0)
    colsum[...] = jnp.broadcast_to(jnp.sum(s, axis=1, keepdims=True), colsum.shape)
    g = lax.dot_general(s, s, NT, precision=HI, preferred_element_type=F32)
    if genes:
        gram[:, :genes] = z_chunk(ncells, 0, genes, packed, colsum, halves, stats)
    gram[:, genes:] = jnp.concatenate([g, g], axis=1)


def eliminate(a, k0, k1):
    rank = a.shape[0]
    a = a.reshape(rank // 8, 8, 2 * rank)
    row = 8 * lax.broadcasted_iota(jnp.int32, a.shape, 0)
    row = row + lax.broadcasted_iota(jnp.int32, a.shape, 1)

    def wide(x):
        return jnp.broadcast_to(x, a.shape[1:])

    for k in range(k0, k1, 8):
        block = a[k // 8]
        p = [wide(block[j : j + 1, :]) for j in range(8)]
        s = [[wide(block[i : i + 1, k + j : k + j + 1]) for j in range(8)] for i in range(8)]
        c = [jnp.broadcast_to(a[:, :, k + j : k + j + 1], a.shape) for j in range(8)]
        for j in range(8):
            r = 1.0 / s[j][j]
            f = c[j] * r[None]
            for t in range(j + 1, 8):
                l = s[t][j] * r
                p[t] = p[t] - l * p[j]
                for u in range(j + 1, 8):
                    s[t][u] = s[t][u] - l * s[j][u]
                c[t] = c[t] - f * s[j][t][None]
            a = a - jnp.where(row > k + j, f, 0.0) * p[j][None]
    return a.reshape(rank, 2 * rank)


def with_identity(gram):
    rank = gram.shape[0]
    lane = lax.broadcasted_iota(jnp.int32, (rank, 2 * rank), 1)
    row = lax.broadcasted_iota(jnp.int32, (rank, 2 * rank), 0)
    return jnp.where(lane < rank, gram, jnp.where(lane - rank == row, 1.0, 0.0))


def lower_inverse(a):
    rank = a.shape[0]
    lane = lax.broadcasted_iota(jnp.int32, (rank, rank), 1)
    row = lax.broadcasted_iota(jnp.int32, (rank, rank), 0)
    diag = jnp.sum(jnp.where(lane == row, a[:, :rank], 0.0), axis=1, keepdims=True)
    return a[:, rank:] * (1.0 / jnp.sqrt(diag))


def inverse_kernel(gram, inverse):
    rank = gram.shape[0]
    inverse[...] = lower_inverse(eliminate(with_identity(gram[...]), 0, rank))


def dot_hi(x, y, dims):
    return lax.dot_general(x, y, dims, precision=HI, preferred_element_type=F32)


def scores_kernel(ncells, sketch, inverse, scores):
    s = lax.dot_general(inverse[...], sketch[...], NN, precision=HI, preferred_element_type=F32)
    scores[...] = s * (float(ncells) ** 0.5)


def z_chunk(ncells, c0, nc, packed, colsum, halves, stats):
    rank = colsum.shape[0]
    half = packed.shape[1] // 2
    cols = slice(c0, c0 + nc)
    z = None
    for i, part in enumerate(halves):
        at = (i // 2) * half
        d = jnp.dot(packed[:, at : at + half], part[:, cols], preferred_element_type=F32)
        z = d if z is None else z + d
    mean, scale = mean_scale(stats[:, cols], ncells)
    return (z[:rank] + z[rank:] - colsum[:, 0:1] * mean) * scale


def product_kernel(ncells, packed, colsum, high0, low0, high1, low1, stats, z):
    n = high0.shape[1]
    nc = min(n, 512)
    halves = (high0, low0, high1, low1)
    for c0 in range(0, n, nc):
        z[:, c0 : c0 + nc] = z_chunk(ncells, c0, nc, packed, colsum, halves, stats)


def dot_parts(x, y, dims):
    xh, xl = two_parts(x)
    yh, yl = two_parts(y)

    def dot(a, b):
        return lax.dot_general(a, b, dims, preferred_element_type=F32)

    return dot(xh, yh) + (dot(xh, yl) + dot(xl, yh))


def finish_kernel(z, inverse, loadings, square):
    l = dot_parts(inverse[...], z[...], NN)
    loadings[...] = l
    square[...] = dot_parts(l, l, NT)


def layout(n):
    tiles = n // 128 + 1
    share = [s * tiles / sum(SHARES) for s in SHARES]
    edges = [round(sum(share[:i])) for i in range(len(share) + 1)]
    sizes = [128 * (b - a) for a, b in zip(edges, edges[1:])]
    return [sizes[0] - 128] + sizes[1:]


def loadings_on_a_line(ncells, sketch, packed, colsum, first, halves, stats):
    rank, n, m = colsum.shape[0], stats.shape[1], sketch.shape[1]
    (lag1, lag2, back), count = LAGS, len(SHARES)
    far = [(i, i ^ 2) for i in range(4)]
    genes = layout(n)
    width = [genes[0] + 2 * rank] + genes[1:]
    begin = [sum(genes[:i]) for i in range(count)]
    pairs = [(0, 1), (1, 0), (2, 3), (3, 2)]
    middle = [(2, 4), (4, 2), (3, 5), (5, 3), (0, 1), (1, 0), (6, 7), (7, 6)]

    slots = count + lag2
    steps = {count + FROM + i: pair for i, pair in enumerate(zip(STEPS, STEPS[1:]))}
    inverted = max(steps)

    def has(i):
        return 0 <= i < count

    def direct(i):
        return count - TAIL <= i < count

    def returns(i):
        return 0 <= i < count - TAIL

    early = {1 + i: count - TAIL + i for i in range(TAIL)}
    finishes, queue = {}, []
    for s in range(slots):
        queue += [d for d in range(count) if d + (lag2 if direct(d) else back) == s]
        take = len(queue) if s > inverted else 0
        finishes[s], queue = queue[:take], queue[take:]

    def chunk(x):
        return jax.ShapeDtypeStruct((rank, x), F32)

    def run(name, ins, outs, kernel):
        def wrapped(*refs):
            kernel(dict(zip(ins, refs)), dict(zip(outs, refs[len(ins) :])))

        results = pl.pallas_call(
            wrapped,
            name=name,
            out_shape=tuple(outs.values()),
            in_specs=[VM] * len(ins),
            out_specs=(VM,) * len(outs),
            compiler_params=params(8),
            cost_estimate=cost(1e9, 1 << 16),
        )(*[val[k] for k in ins])
        val.update(zip(outs, results))

    def at_end():
        z = lax.axis_index("cells")
        return jnp.logical_or(z == 0, z == 3)

    def arrived(d, r):
        if direct(d):
            return r[f"t{d}"][...]
        return jnp.where(at_end(), r[f"down{d}"][:, : width[d]], r[f"t{d}"][...])

    token = jax.ShapeDtypeStruct((8, 128), F32)
    val = dict(token=jnp.zeros((8, 128), F32), square=jnp.zeros((rank, rank), F32))
    val.update(packed=packed, colsum=colsum, stats=stats, z0=first, sketch=sketch)
    val.update(zip(PARTS, halves))

    def main_slot(s, a, b, c):
        ins, outs = ["token"], {"token": token}
        if has(a):
            ins += [f"z{a}"]
        if has(b):
            ins += [f"z{b}", f"up{b}"] + ([f"early{b}"] if direct(b) else [])
            outs[f"s{b}"] = chunk(width[b])
        if has(c):
            ins += [f"s{c}", f"across{c}"]
            outs[f"t{c}"] = chunk(width[c])
        lower = width[c] if returns(c) else width[early[s]] if s in early else 0
        if s in early:
            ins += [f"z{early[s]}"]
        if has(a):
            outs[f"give{s}"] = chunk(max(lower, width[a]))
        if returns(s - back):
            ins += [f"down{s - back}"]

        def kernel(r, o):
            o["token"][...] = r["token"][...]
            if has(b):
                came = r[f"up{b}"][:, : width[b]]
                if direct(b):
                    came = jnp.where(at_end(), r[f"early{b}"][:, : width[b]], came)
                o[f"s{b}"][...] = r[f"z{b}"][...] + came
            if has(c):
                tt = r[f"s{c}"][...] + r[f"across{c}"][...]
                o[f"t{c}"][...] = tt
            if has(a) and lower:
                zz, give = r[f"z{a}"], o[f"give{s}"]
                low = tt if returns(c) else r[f"z{early[s]}"][...]
                least = min(width[a], lower)
                give[:, :least] = jnp.where(at_end(), zz[:, :least], low[:, :least])
                if width[a] > least:
                    give[:, least:] = zz[:, least:]
                if lower > least:
                    give[:, least:] = low[:, least:]
            elif has(a):
                o[f"give{s}"][...] = r[f"z{a}"][...]

        if s:
            run(f"slot{s}", ins, outs, kernel)
        if f"give{s}" in val:
            return val[f"give{s}"]
        return val[f"z{a}"] if has(a) else val[f"t{c}"] if returns(c) else None

    def side_slot(s, a):
        ins, outs = ["token"], {"token": token}
        made = [a] if has(a) and not direct(a) else []
        made += [early[a]] if a in early else []
        if made:
            ins += ["packed", "colsum", "stats", *PARTS]
        for i in made:
            outs[f"z{i}"] = chunk(width[i])
        if s in steps:
            ins += ["t0", "down0"] if steps[s][0] == 0 else ["state"]
            if s == inverted:
                outs["inverse"] = chunk(rank)
            else:
                outs["state"] = chunk(2 * rank)
        if finishes[s]:
            for d in finishes[s]:
                ins += [f"t{d}"] if direct(d) else [f"t{d}", f"down{d}"]
                outs[f"l{d}"] = chunk(genes[d])
            ins += ["square"] if s == inverted else ["inverse", "square"]
            outs["square"] = chunk(rank)
        ins = list(dict.fromkeys(ins))

        def kernel(r, o):
            o["token"][...] = r["token"][...]
            for i in made:
                o[f"z{i}"][...] = z_chunk(
                    ncells,
                    begin[i],
                    genes[i],
                    r["packed"],
                    r["colsum"],
                    [r[k] for k in PARTS],
                    r["stats"],
                )
            if s in steps:
                if steps[s][0] == 0:
                    x = with_identity(arrived(0, r)[:, -2 * rank :])
                else:
                    x = r["state"][...]
                x = eliminate(x, *steps[s])
                if s == inverted:
                    x = lower_inverse(x)
                    o["inverse"][...] = x
                else:
                    o["state"][...] = x
            if finishes[s]:
                total = r["square"][...]
                inverse = x if s == inverted else r["inverse"][...]
                for d in finishes[s]:
                    l = dot_parts(inverse, arrived(d, r)[:, : genes[d]], NN)
                    o[f"l{d}"][...] = l
                    total = total + dot_parts(l, l, NT)
                o["square"][...] = total

        if len(outs) > 1:
            run(f"side{s}", ins, outs, kernel)

    for s in range(slots):
        a, b, c = s, s - lag1, s - lag2
        give = main_slot(s, a, b, c)
        if give is not None:
            got = lax.ppermute(give, "cells", pairs)
            if has(a):
                val[f"up{a}"] = got
            if s in early:
                val[f"early{early[s]}"] = got
            if returns(c):
                val[f"down{c}"] = got
        if has(b) and direct(b):
            val[f"across{b}"] = lax.ppermute(val[f"s{b}"], "cells", far)
        elif has(b):
            val[f"across{b}"] = lax.ppermute(val[f"s{b}"], ("cells", "sub"), middle)
        side_slot(s, a + 1)

    def last(r, o):
        o["scores"][...] = dot_parts(r["inverse"][...], r["sketch"][...], NN) * (
            float(ncells) ** 0.5
        )
        for d in range(count):
            o["loadings"][:, begin[d] : begin[d] + genes[d]] = r[f"l{d}"][...]

    pieces = [f"l{d}" for d in range(count)]
    run("last", ["token", "inverse", "sketch"] + pieces, dict(scores=chunk(m), loadings=chunk(n)), last)
    return val["loadings"], val["square"], val["scores"]


PARTS = ("high0", "low0", "high1", "low1")
LAGS = (2, 4, 6)
TAIL = 2
SHARES = (3, 4, 4, 4, 4, 4, 4, 3, 3)
STEPS = (0, 64)
FROM = 1


def call(kernel, name, out_shape, args, scratch=(), mib=4, flops=0, nbytes=MIB):
    single = not isinstance(out_shape, tuple)
    return pl.pallas_call(
        kernel,
        name=name,
        out_shape=out_shape,
        in_specs=[VM] * len(args),
        out_specs=VM if single else (VM,) * len(out_shape),
        scratch_shapes=list(scratch),
        compiler_params=params(mib),
        cost_estimate=cost(flops, nbytes),
    )(*args)


def f32(*shape):
    return jax.ShapeDtypeStruct(shape, F32)


def body(counts, start_block):
    m, n = counts.shape
    rank = start_block.shape[1]
    cells = lax.axis_size("cells")
    ncells = m * cells
    genes = n * lax.axis_size("genes") * lax.axis_size("sub")

    bm = 128
    held, total = pl.pallas_call(
        functools.partial(totals_kernel, bm),
        name="totals",
        out_shape=(pltpu.VMEM((m, n), jnp.int32), f32(1, m)),
        in_specs=[pl.BlockSpec(memory_space=pltpu.HBM)],
        out_specs=(VM, VM),
        scratch_shapes=[pltpu.SemaphoreType.DMA((m // bm,))],
        compiler_params=params(4),
        cost_estimate=cost(0, 24 * m * n),
    )(pltpu.with_memory_space_constraint(counts, pltpu.HBM))
    library = sum_of_four(total, ("genes", "sub"))

    logged, stats = call(
        stats_kernel,
        "stats",
        (pltpu.VMEM((m, n), F32), f32(2, n)),
        [vmem(held), library],
        [pltpu.VMEM((m, 128), F32)],
        nbytes=20 * m * n,
    )
    logged = vmem(logged)

    halves = []
    for i in range(2):
        halves += call(
            functools.partial(split_kernel, i * (m // 2)),
            "split",
            (pltpu.VMEM((m // 2, n), BF16), pltpu.VMEM((m // 2, n), BF16)),
            [logged],
            nbytes=4 * m * n,
        )
    stats = sum_of_four(stats, ("cells",))

    halves = [vmem(x) for x in halves]
    away, weight, shift = call(
        functools.partial(away_kernel, ncells),
        "away",
        (f32(2, rank, m // 4), jax.ShapeDtypeStruct((n, 2 * rank), BF16), f32(rank, 128)),
        [*halves, start_block.T, stats],
        flops=4 * m * n * rank,
        mib=8,
    )
    away = swap(away, "sub")
    part = call(
        own_kernel,
        "own",
        f32(2, rank, m // 4),
        [*halves, weight, shift],
        flops=4 * m * n * rank,
        mib=8,
    )
    own, other = [], []
    for i in range(2):
        own.append(sum_over(part[i] + away[i], ("genes",)))
        other.append(swap(own[i], "sub"))

    line = cells == 4 and n % 1024 == 0 and 2 * rank == 128
    genes0 = layout(n)[0] if line else 0
    sketch, packed, colsum, gram = call(
        functools.partial(prep_kernel, ncells, genes0),
        "prep",
        (
            f32(rank, m),
            jax.ShapeDtypeStruct((2 * rank, m), BF16),
            f32(rank, 128),
            f32(rank, genes0 + 2 * rank),
        ),
        own + other + ([*halves, stats] if line else []),
        flops=12 * m * rank * rank,
        mib=8,
    )

    if line:
        loadings, square, scores = loadings_on_a_line(
            ncells, sketch, packed, colsum, gram, halves, stats
        )
    else:
        z = call(
            functools.partial(product_kernel, ncells),
            "product",
            f32(rank, n),
            [packed, colsum, *halves, stats],
            mib=8,
        )
        inverse = call(
            inverse_kernel, "inverse", f32(rank, rank), [sum_over(gram, ("cells",))]
        )
        loadings, square = call(
            finish_kernel,
            "finish",
            (f32(rank, n), f32(rank, rank)),
            [lax.psum(z, "cells"), inverse],
            mib=16,
        )
        scores = call(
            functools.partial(scores_kernel, ncells), "scores", f32(rank, m), [sketch, inverse]
        )
    ritz = sum_of_four(square, ("genes", "sub")) / genes
    return (scores.T, loadings.T, ritz)


def solution(mesh):
    placed = (P(("groups", "cells"), ("genes", "sub")), P(("genes", "sub"), None))
    return jax.shard_map(
        body,
        mesh=mesh,
        in_specs=placed,
        out_specs=(
            P(("groups", "cells"), None),
            P(("groups", "genes", "sub"), None),
            P("groups", None),
        ),
        check_vma=False,
    )
```

```python
import functools

import jax
import jax.numpy as jnp
from jax import lax
from jax.experimental import pallas as pl
from jax.experimental.pallas import tpu as pltpu
from jax.sharding import PartitionSpec as P

F32 = jnp.float32
BF16 = jnp.bfloat16
HI = lax.Precision.HIGHEST
VM = pl.BlockSpec(memory_space=pltpu.VMEM)
SM = pl.BlockSpec(memory_space=pltpu.SMEM)
ANY = pl.BlockSpec(memory_space=pl.ANY)
MIB = 1 << 20
LN2 = 0.6931471805599453
NT = (((1,), (1,)), ((), ()))
NN = (((1,), (0,)), ((), ()))


def params(mib=16):
    return pltpu.CompilerParams(vmem_limit_bytes=mib * MIB)


def vmem(x):
    return pltpu.with_memory_space_constraint(x, pltpu.VMEM)


def cost(flops, nbytes):
    return pl.CostEstimate(flops=int(flops), bytes_accessed=int(nbytes), transcendentals=0)


def swap(x, axis, k=1):
    size = lax.axis_size(axis)
    return lax.ppermute(x, axis, [(i, i ^ k) for i in range(size)])


def is_pow2(size):
    return size & (size - 1) == 0


def sum_over(x, axes):
    for axis in axes:
        size = lax.axis_size(axis)
        if not is_pow2(size):
            x = lax.psum(x, axis)
            continue
        k = 1
        while k < size:
            x = x + swap(x, axis, k)
            k *= 2
    return x


def sum_of_four(x, axes):
    size = 1
    for axis in axes:
        size *= lax.axis_size(axis)
    if size != 4:
        return sum_over(x, axes[::-1])
    c, b, a = (lax.ppermute(x, axes, [(i, i ^ k) for i in range(4)]) for k in (3, 2, 1))
    return (c + b) + (a + x)


def totals_kernel(bm, counts, held, total, sem):
    m, n = counts.shape

    blocks = [(i, bm) for i in range(0, m - bm, bm)]
    blocks += [(m - bm, bm // 2), (m - bm // 2, bm // 4), (m - bm // 4, bm // 4)]

    def fetch(i):
        rows = pl.ds(*blocks[i])
        return pltpu.make_async_copy(counts.at[rows, :], held.at[rows, :], sem.at[i])

    for i in range(len(blocks)):
        fetch(i).start()
    parts = []
    for i, (at, size) in enumerate(blocks):
        fetch(i).wait()

        def tile(t, acc, at=at, size=size):
            return acc + held[pl.ds(at, size), pl.ds(pl.multiple_of(t * 128, 128), 128)]

        zero = jnp.zeros((size, 128), jnp.int32)
        parts.append(lax.fori_loop(0, n // 128, tile, zero, unroll=8).astype(F32))
        if (at + size) % 128 == 0:
            acc = jnp.concatenate(parts, axis=0)
            parts = []
            total[:, at + size - 128 : at + size] = jnp.sum(acc.T, axis=0, keepdims=True)


def column(library, factor, m):
    for t in range(m // 128):
        row = 10000.0 / library[:, t * 128 : (t + 1) * 128]
        factor[t * 128 : (t + 1) * 128, :] = jnp.broadcast_to(row, (128, 128)).T


def stats_kernel(held, library, logged, stats, factor):
    m, n = held.shape
    column(library, factor, m)
    width = 512

    def over_cols(t, carry):
        cols = pl.ds(pl.multiple_of(t * width, width), width)
        s = jnp.concatenate([factor[...]] * (width // 128), axis=1)
        y = jnp.log2(1.0 + held[:, cols].astype(F32) * s)
        logged[:, cols] = y
        parts = y.reshape(m // 8, 8, width)
        one, two = jnp.sum(parts, axis=0), jnp.sum(parts * parts, axis=0)
        stats[0:1, cols] = jnp.sum(one, axis=0, keepdims=True)
        stats[1:2, cols] = jnp.sum(two, axis=0, keepdims=True)
        return carry

    lax.fori_loop(0, n // width, over_cols, 0)


def two_parts(x):
    h = x.astype(BF16)
    return h, (x - h.astype(F32)).astype(BF16)


def split_kernel(begin, logged, high, low):
    m, n = high.shape
    width, bm = 512, 64

    def over_rows(r, carry):
        rows = pl.ds(pl.multiple_of(r * bm, bm), bm)
        source = pl.ds(pl.multiple_of(begin + r * bm, bm), bm)

        def over_cols(t, c):
            cols = pl.ds(pl.multiple_of(t * width, width), width)
            high[rows, cols], low[rows, cols] = two_parts(logged[source, cols])
            return c

        return lax.fori_loop(0, n // width, over_cols, carry)

    lax.fori_loop(0, m // bm, over_rows, 0)


def mean_scale(stats, ncells):
    mean = stats[0:1, :] / ncells
    meansq = stats[1:2, :] / ncells
    return mean, LN2 / jnp.sqrt((LN2 * LN2) * (meansq - mean * mean) + 1e-05)


def sketch_half(high, low, weight, shift, out):
    rank = weight.shape[1] // 2
    half = high.shape[0]
    both = jnp.concatenate([high[...], low[...]], axis=0)
    acc = jnp.dot(both, weight[...], preferred_element_type=F32)
    acc = (acc[:half] + acc[half:]).T
    acc = acc[:rank] + acc[rank:] - shift[:, 0:1]
    for i in range(2):
        out[i] = acc[:, i * (half // 2) : (i + 1) * (half // 2)]


def away_kernel(ncells, high0, low0, high1, low1, start_t, stats, away, weight, shift):
    mean, scale = mean_scale(stats[...], ncells)
    w = start_t[...] * scale
    shift[...] = jnp.broadcast_to(jnp.sum(w * mean, axis=1, keepdims=True), shift.shape)
    h, l = two_parts(w)
    weight[...] = jnp.concatenate([h, l], axis=0).T
    me = lax.axis_index("sub")
    pl.when(me == 1)(lambda: sketch_half(high0, low0, weight, shift, away))
    pl.when(me == 0)(lambda: sketch_half(high1, low1, weight, shift, away))


def own_kernel(high0, low0, high1, low1, weight, shift, own):
    me = lax.axis_index("sub")
    pl.when(me == 0)(lambda: sketch_half(high0, low0, weight, shift, own))
    pl.when(me == 1)(lambda: sketch_half(high1, low1, weight, shift, own))


def prep_kernel(ncells, genes, *refs):
    own0, own1, other0, other1 = refs[:4]
    if genes:
        halves, stats = refs[4:8], refs[8]
    sketch, packed, colsum, gram = refs[-4:]
    rank = own0.shape[0]
    mine = jnp.concatenate([own0[...], own1[...]], axis=1)
    theirs = jnp.concatenate([other0[...], other1[...]], axis=1)
    first = lax.axis_index("sub") == 0
    s = jnp.concatenate([jnp.where(first, mine, theirs), jnp.where(first, theirs, mine)], axis=1)
    sketch[...] = s
    h, l = two_parts(s)
    packed[...] = jnp.concatenate([h, l], axis=0)
    colsum[...] = jnp.broadcast_to(jnp.sum(s, axis=1, keepdims=True), colsum.shape)
    g = lax.dot_general(s, s, NT, precision=HI, preferred_element_type=F32)
    if genes:
        gram[:, :genes] = z_chunk(ncells, 0, genes, packed, colsum, halves, stats)
    gram[:, genes:] = jnp.concatenate([g, g], axis=1)


def eliminate(a, k0, k1):
    rank = a.shape[0]
    a = a.reshape(rank // 8, 8, 2 * rank)
    row = 8 * lax.broadcasted_iota(jnp.int32, a.shape, 0)
    row = row + lax.broadcasted_iota(jnp.int32, a.shape, 1)

    def wide(x):
        return jnp.broadcast_to(x, a.shape[1:])

    for k in range(k0, k1, 8):
        block = a[k // 8]
        p = [wide(block[j : j + 1, :]) for j in range(8)]
        s = [[wide(block[i : i + 1, k + j : k + j + 1]) for j in range(8)] for i in range(8)]
        c = [jnp.broadcast_to(a[:, :, k + j : k + j + 1], a.shape) for j in range(8)]
        for j in range(8):
            r = 1.0 / s[j][j]
            f = c[j] * r[None]
            for t in range(j + 1, 8):
                l = s[t][j] * r
                p[t] = p[t] - l * p[j]
                for u in range(j + 1, 8):
                    s[t][u] = s[t][u] - l * s[j][u]
                c[t] = c[t] - f * s[j][t][None]
            a = a - jnp.where(row > k + j, f, 0.0) * p[j][None]
    return a.reshape(rank, 2 * rank)


def with_identity(gram):
    rank = gram.shape[0]
    lane = lax.broadcasted_iota(jnp.int32, (rank, 2 * rank), 1)
    row = lax.broadcasted_iota(jnp.int32, (rank, 2 * rank), 0)
    return jnp.where(lane < rank, gram, jnp.where(lane - rank == row, 1.0, 0.0))


def lower_inverse(a):
    rank = a.shape[0]
    lane = lax.broadcasted_iota(jnp.int32, (rank, rank), 1)
    row = lax.broadcasted_iota(jnp.int32, (rank, rank), 0)
    diag = jnp.sum(jnp.where(lane == row, a[:, :rank], 0.0), axis=1, keepdims=True)
    return a[:, rank:] * (1.0 / jnp.sqrt(diag))


def inverse_kernel(gram, inverse):
    rank = gram.shape[0]
    inverse[...] = lower_inverse(eliminate(with_identity(gram[...]), 0, rank))


def dot_hi(x, y, dims):
    return lax.dot_general(x, y, dims, precision=HI, preferred_element_type=F32)


def scores_kernel(ncells, sketch, inverse, scores):
    s = lax.dot_general(inverse[...], sketch[...], NN, precision=HI, preferred_element_type=F32)
    scores[...] = s * (float(ncells) ** 0.5)


def z_chunk(ncells, c0, nc, packed, colsum, halves, stats):
    rank = colsum.shape[0]
    half = packed.shape[1] // 2
    cols = slice(c0, c0 + nc)
    z = None
    for i, part in enumerate(halves):
        at = (i // 2) * half
        d = jnp.dot(packed[:, at : at + half], part[:, cols], preferred_element_type=F32)
        z = d if z is None else z + d
    mean, scale = mean_scale(stats[:, cols], ncells)
    return (z[:rank] + z[rank:] - colsum[:, 0:1] * mean) * scale


def product_kernel(ncells, packed, colsum, high0, low0, high1, low1, stats, z):
    n = high0.shape[1]
    nc = min(n, 512)
    halves = (high0, low0, high1, low1)
    for c0 in range(0, n, nc):
        z[:, c0 : c0 + nc] = z_chunk(ncells, c0, nc, packed, colsum, halves, stats)


def dot_parts(x, y, dims):
    xh, xl = two_parts(x)
    yh, yl = two_parts(y)

    def dot(a, b):
        return lax.dot_general(a, b, dims, preferred_element_type=F32)

    return dot(xh, yh) + (dot(xh, yl) + dot(xl, yh))


def finish_kernel(z, inverse, loadings, square):
    l = dot_parts(inverse[...], z[...], NN)
    loadings[...] = l
    square[...] = dot_parts(l, l, NT)


def layout(n):
    tiles = n // 128 + 1
    share = [s * tiles / sum(SHARES) for s in SHARES]
    edges = [round(sum(share[:i])) for i in range(len(share) + 1)]
    sizes = [128 * (b - a) for a, b in zip(edges, edges[1:])]
    return [sizes[0] - 128] + sizes[1:]


def loadings_on_a_line(ncells, sketch, packed, colsum, first, halves, stats):
    rank, n, m = colsum.shape[0], stats.shape[1], sketch.shape[1]
    (lag1, lag2, back), count = LAGS, len(SHARES)
    far = [(i, i ^ 2) for i in range(4)]
    genes = layout(n)
    width = [genes[0] + 2 * rank] + genes[1:]
    begin = [sum(genes[:i]) for i in range(count)]
    pairs = [(0, 1), (1, 0), (2, 3), (3, 2)]
    middle = [(2, 4), (4, 2), (3, 5), (5, 3), (0, 1), (1, 0), (6, 7), (7, 6)]

    slots = count + lag2
    steps = {count + FROM + i: pair for i, pair in enumerate(zip(STEPS, STEPS[1:]))}
    inverted = max(steps)

    def has(i):
        return 0 <= i < count

    def direct(i):
        return count - TAIL <= i < count

    def returns(i):
        return 0 <= i < count - TAIL

    early = {1 + i: count - TAIL + i for i in range(TAIL)}
    finishes, queue = {}, []
    for s in range(slots):
        queue += [d for d in range(count) if d + (lag2 if direct(d) else back) == s]
        take = len(queue) if s > inverted else 0
        finishes[s], queue = queue[:take], queue[take:]

    def chunk(x):
        return jax.ShapeDtypeStruct((rank, x), F32)

    def run(name, ins, outs, kernel):
        def wrapped(*refs):
            kernel(dict(zip(ins, refs)), dict(zip(outs, refs[len(ins) :])))

        results = pl.pallas_call(
            wrapped,
            name=name,
            out_shape=tuple(outs.values()),
            in_specs=[VM] * len(ins),
            out_specs=(VM,) * len(outs),
            compiler_params=params(8),
            cost_estimate=cost(2e8, 1 << 16),
        )(*[val[k] for k in ins])
        val.update(zip(outs, results))

    def at_end():
        z = lax.axis_index("cells")
        return jnp.logical_or(z == 0, z == 3)

    def arrived(d, r):
        if direct(d):
            return r[f"t{d}"][...]
        return jnp.where(at_end(), r[f"down{d}"][:, : width[d]], r[f"t{d}"][...])

    token = jax.ShapeDtypeStruct((8, 128), F32)
    val = dict(token=jnp.zeros((8, 128), F32), square=jnp.zeros((rank, rank), F32))
    val.update(packed=packed, colsum=colsum, stats=stats, z0=first, sketch=sketch)
    val.update(zip(PARTS, halves))

    def merge(give, upper, lower):
        up, low = upper.shape[1], lower.shape[1]
        least = min(up, low)
        give[:, :least] = jnp.where(at_end(), upper[:, :least], lower[:, :least])
        if up > least:
            give[:, least:] = upper[:, least:]
        if low > least:
            give[:, least:] = lower[:, least:]

    def main_slot(s, a, b, c):
        ins, outs = ["token"], {"token": token}
        if has(a):
            ins += [f"z{a}"]
        if has(b):
            ins += [f"z{b}", f"up{b}"] + ([f"early{b}"] if direct(b) else [])
            outs[f"s{b}"] = chunk(width[b])
        if has(c):
            ins += [f"s{c}", f"across{c}"]
            outs[f"t{c}"] = chunk(width[c])
        lower = width[c] if returns(c) else 0
        if has(a) and s >= lag2:
            outs[f"give{s}"] = chunk(max(lower, width[a]))
        if returns(s - back):
            ins += [f"down{s - back}"]

        def kernel(r, o):
            o["token"][...] = r["token"][...]
            if has(b):
                came = r[f"up{b}"][:, : width[b]]
                if direct(b):
                    came = jnp.where(at_end(), r[f"early{b}"][:, : width[b]], came)
                o[f"s{b}"][...] = r[f"z{b}"][...] + came
            if has(c):
                tt = r[f"s{c}"][...] + r[f"across{c}"][...]
                o[f"t{c}"][...] = tt
            if f"give{s}" in o and lower:
                merge(o[f"give{s}"], r[f"z{a}"], tt)
            elif f"give{s}" in o:
                o[f"give{s}"][...] = r[f"z{a}"][...]

        if has(b) or has(c):
            run(f"slot{s}", ins, outs, kernel)
        if f"give{s}" in val:
            return val[f"give{s}"]
        return val[f"z{a}"] if has(a) else val[f"t{c}"] if returns(c) else None

    def side_slot(s, a):
        ins, outs = ["token"], {"token": token}
        made = [a] if has(a) and not direct(a) else []
        made += [early[a]] if a in early else []
        if made:
            ins += ["packed", "colsum", "stats", *PARTS]
        for i in made:
            outs[f"z{i}"] = chunk(width[i])
        if a in early:
            outs[f"give{a}"] = chunk(max(width[i] for i in made))
        if s in steps:
            ins += ["t0", "down0"] if steps[s][0] == 0 else ["state"]
            if s == inverted:
                outs["inverse"] = chunk(rank)
            else:
                outs["state"] = chunk(2 * rank)
        if finishes[s]:
            for d in finishes[s]:
                ins += [f"t{d}"] if direct(d) else [f"t{d}", f"down{d}"]
                outs[f"l{d}"] = chunk(genes[d])
            ins += ["square"] if s == inverted else ["inverse", "square"]
            outs["square"] = chunk(rank)
        ins = list(dict.fromkeys(ins))

        def kernel(r, o):
            o["token"][...] = r["token"][...]
            for i in made:
                o[f"z{i}"][...] = z_chunk(
                    ncells,
                    begin[i],
                    genes[i],
                    r["packed"],
                    r["colsum"],
                    [r[k] for k in PARTS],
                    r["stats"],
                )
            if a in early:
                merge(o[f"give{a}"], o[f"z{a}"], o[f"z{early[a]}"])
            if s in steps:
                if steps[s][0] == 0:
                    x = with_identity(arrived(0, r)[:, -2 * rank :])
                else:
                    x = r["state"][...]
                x = eliminate(x, *steps[s])
                if s == inverted:
                    x = lower_inverse(x)
                    o["inverse"][...] = x
                else:
                    o["state"][...] = x
            if finishes[s]:
                total = r["square"][...]
                inverse = x if s == inverted else r["inverse"][...]
                z = [arrived(d, r)[:, : genes[d]] for d in finishes[s]]
                l = dot_parts(inverse, jnp.concatenate(z, axis=1), NN)
                at = 0
                for d in finishes[s]:
                    o[f"l{d}"][...] = l[:, at : at + genes[d]]
                    at += genes[d]
                o["square"][...] = total + dot_parts(l, l, NT)

        if len(outs) > 1:
            run(f"side{s}", ins, outs, kernel)

    for s in range(slots):
        a, b, c = s, s - lag1, s - lag2
        give = main_slot(s, a, b, c)
        if give is not None:
            got = lax.ppermute(give, "cells", pairs)
            if has(a):
                val[f"up{a}"] = got
            if s in early:
                val[f"early{early[s]}"] = got
            if returns(c):
                val[f"down{c}"] = got
        if has(b) and direct(b):
            val[f"across{b}"] = lax.ppermute(val[f"s{b}"], "cells", far)
        elif has(b):
            val[f"across{b}"] = lax.ppermute(val[f"s{b}"], ("cells", "sub"), middle)
        side_slot(s, a + 1)

    def last(r, o):
        o["scores"][...] = dot_parts(r["inverse"][...], r["sketch"][...], NN) * (
            float(ncells) ** 0.5
        )
        for d in range(count):
            o["loadings"][:, begin[d] : begin[d] + genes[d]] = r[f"l{d}"][...]

    pieces = [f"l{d}" for d in range(count)]
    run("last", ["token", "inverse", "sketch"] + pieces, dict(scores=chunk(m), loadings=chunk(n)), last)
    return val["loadings"], val["square"], val["scores"]


PARTS = ("high0", "low0", "high1", "low1")
LAGS = (2, 4, 6)
TAIL = 2
SHARES = (3, 4, 4, 4, 4, 4, 4, 3, 3)
STEPS = (0, 64)
FROM = 1


def call(kernel, name, out_shape, args, scratch=(), mib=4, flops=0, nbytes=MIB):
    single = not isinstance(out_shape, tuple)
    return pl.pallas_call(
        kernel,
        name=name,
        out_shape=out_shape,
        in_specs=[VM] * len(args),
        out_specs=VM if single else (VM,) * len(out_shape),
        scratch_shapes=list(scratch),
        compiler_params=params(mib),
        cost_estimate=cost(flops, nbytes),
    )(*args)


def f32(*shape):
    return jax.ShapeDtypeStruct(shape, F32)


def body(counts, start_block):
    m, n = counts.shape
    rank = start_block.shape[1]
    cells = lax.axis_size("cells")
    ncells = m * cells
    genes = n * lax.axis_size("genes") * lax.axis_size("sub")

    bm = 128
    held, total = pl.pallas_call(
        functools.partial(totals_kernel, bm),
        name="totals",
        out_shape=(pltpu.VMEM((m, n), jnp.int32), f32(1, m)),
        in_specs=[pl.BlockSpec(memory_space=pltpu.HBM)],
        out_specs=(VM, VM),
        scratch_shapes=[pltpu.SemaphoreType.DMA((m // bm + 2,))],
        compiler_params=params(4),
        cost_estimate=cost(0, 24 * m * n),
    )(pltpu.with_memory_space_constraint(counts, pltpu.HBM))
    library = sum_of_four(total, ("genes", "sub"))

    logged, stats = call(
        stats_kernel,
        "stats",
        (pltpu.VMEM((m, n), F32), f32(2, n)),
        [vmem(held), library],
        [pltpu.VMEM((m, 128), F32)],
        nbytes=20 * m * n,
    )
    logged = vmem(logged)

    halves = []
    for i in range(2):
        halves += call(
            functools.partial(split_kernel, i * (m // 2)),
            "split",
            (pltpu.VMEM((m // 2, n), BF16), pltpu.VMEM((m // 2, n), BF16)),
            [logged],
            nbytes=4 * m * n,
        )
    stats = sum_of_four(stats, ("cells",))

    halves = [vmem(x) for x in halves]
    away, weight, shift = call(
        functools.partial(away_kernel, ncells),
        "away",
        (f32(2, rank, m // 4), jax.ShapeDtypeStruct((n, 2 * rank), BF16), f32(rank, 128)),
        [*halves, start_block.T, stats],
        flops=4 * m * n * rank,
        mib=8,
    )
    away = swap(away, "sub")
    part = call(
        own_kernel,
        "own",
        f32(2, rank, m // 4),
        [*halves, weight, shift],
        flops=4 * m * n * rank,
        mib=8,
    )
    own, other = [], []
    for i in range(2):
        own.append(sum_over(part[i] + away[i], ("genes",)))
        other.append(swap(own[i], "sub"))

    line = cells == 4 and n % 1024 == 0 and 2 * rank == 128
    genes0 = layout(n)[0] if line else 0
    sketch, packed, colsum, gram = call(
        functools.partial(prep_kernel, ncells, genes0),
        "prep",
        (
            f32(rank, m),
            jax.ShapeDtypeStruct((2 * rank, m), BF16),
            f32(rank, 128),
            f32(rank, genes0 + 2 * rank),
        ),
        own + other + ([*halves, stats] if line else []),
        flops=12 * m * rank * rank,
        mib=8,
    )

    if line:
        loadings, square, scores = loadings_on_a_line(
            ncells, sketch, packed, colsum, gram, halves, stats
        )
    else:
        z = call(
            functools.partial(product_kernel, ncells),
            "product",
            f32(rank, n),
            [packed, colsum, *halves, stats],
            mib=8,
        )
        inverse = call(
            inverse_kernel, "inverse", f32(rank, rank), [sum_over(gram, ("cells",))]
        )
        loadings, square = call(
            finish_kernel,
            "finish",
            (f32(rank, n), f32(rank, rank)),
            [lax.psum(z, "cells"), inverse],
            mib=16,
        )
        scores = call(
            functools.partial(scores_kernel, ncells), "scores", f32(rank, m), [sketch, inverse]
        )
    ritz = sum_of_four(square, ("genes", "sub")) / genes
    return (scores.T, loadings.T, ritz)


def solution(mesh):
    placed = (P(("groups", "cells"), ("genes", "sub")), P(("genes", "sub"), None))
    return jax.shard_map(
        body,
        mesh=mesh,
        in_specs=placed,
        out_specs=(
            P(("groups", "cells"), None),
            P(("groups", "genes", "sub"), None),
            P("groups", None),
        ),
        check_vma=False,
    )
```
